32 devices in a mesh: lat: 8 (over y, x, core), lon: 4 (over z).
Axes of the slice: x: 2, y: 2, z: 4, core: 2. Of those that a mesh axis runs over, the one named last changes fastest.
Arguments:
- potential_heat_state: float32 [16, 512, 512], P(None, 'lat', 'lon'), may hold values from -6 to 6
- saltiness_anomaly: float32 [16, 512, 512], P(None, 'lat', 'lon'), may hold values from -6 to 6
- first_current_component: float32 [16, 512, 512], P(None, 'lat', 'lon'), may hold values from -6 to 6
- second_current_component: float32 [16, 512, 512], P(None, 'lat', 'lon'), may hold values from -6 to 6
- bathymetry_layer_total: int32 [512, 512], P('lat', 'lon'), may hold values from 0 to 16
- westeast_cell_extent: float32 [512, 512], P('lat', 'lon'), may hold values from 1 to 2
- southnorth_cell_extent: float32 [512, 512], P('lat', 'lon'), may hold values from 1 to 2
- planetary_vorticity: float32 [512, 512], P('lat', 'lon'), may hold values from -1.5 to 1.5
- scalar_mixing_factor: float32 [16], replicated, may hold values from 0.05 to 0.5
- momentum_mixing_factor: float32 [16], replicated, may hold values from 0.05 to 0.5
Outputs:
- new_temperature: float32 [16, 512, 512], P(None, 'lat', 'lon')
- new_salinity: float32 [16, 512, 512], P(None, 'lat', 'lon')
- new_zonal: float32 [16, 512, 512], P(None, 'lat', 'lon')
- new_north: float32 [16, 512, 512], P(None, 'lat', 'lon')
The draws below stay inside these ranges and needn't reach their ends.
All inputs are finite; a program needn't handle non-finite values.
Results may differ from the reference program's by a relative error of at most 0.00002.
Values sent between devices are 32-bit elements; how exact they have to be, the bound alone decides.
A program may use at most 64 MiB of HBM per device.

```python
import math
import jax
import jax.numpy as jnp
from jax import lax

VERTICAL_LAYERS = 16
STEPS = 3
NORTHWARD_CELLS = 512
CIRCUMFERENCE_N = 512


def touch_ends(result, stream_key, low, largest):
    longest = result.shape.index(max(result.shape))
    spots = []
    for shift in (0, 1):
        where = [jax.random.randint(jax.random.fold_in(stream_key, axis), (), 0, length) for axis, length in enumerate(result.shape)]
        where[longest] = (where[longest] + shift) % result.shape[longest]
        spots.append(tuple(where))
    return result.at[spots[0]].set(low).at[spots[1]].set(largest)


def shard_levels(stream_key, extent, pieces, least, largest):
    level, own = 1.0, jax.random.fold_in(stream_key, 6)
    for axis_at, blocks in pieces:
        heights = jnp.exp(jax.random.uniform(jax.random.fold_in(own, axis_at), (blocks,), jnp.float32, least / len(pieces), largest / len(pieces)))
        level = level * jnp.repeat(heights, extent[axis_at] // blocks).reshape([-1 if axis == axis_at else 1 for axis in range(len(extent))])
    return level


def centred(stream_key, shape, scale, bound, shards=(), held_as=jnp.bfloat16):
    drawn = jax.random.normal(stream_key, shape, jnp.float32) * scale
    if len(shards) > 0:
        drawn = shard_levels(stream_key, shape, shards, -0.22, 0.18) * drawn
    return jnp.clip(drawn, min=-bound, max=bound).astype(held_as)


def setup_inputs(seed: int = 0) -> dict:
    seeds = jax.random.split(jax.random.key(seed), 11)
    return {
        "potential_heat_state": centred(seeds[0], (VERTICAL_LAYERS, NORTHWARD_CELLS, CIRCUMFERENCE_N), 1.0, 6.0, ((1, 8), (2, 4)), jnp.float32),
        "saltiness_anomaly": centred(seeds[1], (VERTICAL_LAYERS, NORTHWARD_CELLS, CIRCUMFERENCE_N), 1.0, 6.0, ((1, 8), (2, 4)), jnp.float32),
        "first_current_component": centred(seeds[2], (VERTICAL_LAYERS, NORTHWARD_CELLS, CIRCUMFERENCE_N), 1.0, 6.0, ((1, 8), (2, 4)), jnp.float32),
        "second_current_component": centred(seeds[3], (VERTICAL_LAYERS, NORTHWARD_CELLS, CIRCUMFERENCE_N), 1.0, 6.0, ((1, 8), (2, 4)), jnp.float32),
        "bathymetry_layer_total": touch_ends(jax.random.randint(seeds[4], (NORTHWARD_CELLS, CIRCUMFERENCE_N), 0, VERTICAL_LAYERS + 1), jax.random.fold_in(seeds[4], 1), 0, VERTICAL_LAYERS).astype(jnp.int32),
        "westeast_cell_extent": jnp.clip(jnp.exp(math.log(2.0) - 0.6931472 * jax.random.uniform(seeds[5], (NORTHWARD_CELLS, CIRCUMFERENCE_N), jnp.float32) ** shard_levels(seeds[5], (NORTHWARD_CELLS, CIRCUMFERENCE_N), ((0, 8), (1, 4)), -0.2, 0.2)), 1.0, 2.0),
        "southnorth_cell_extent": jnp.clip(jnp.exp(math.log(2.0) - 0.6931472 * jax.random.uniform(seeds[6], (NORTHWARD_CELLS, CIRCUMFERENCE_N), jnp.float32) ** shard_levels(seeds[6], (NORTHWARD_CELLS, CIRCUMFERENCE_N), ((0, 8), (1, 4)), -0.2, 0.2)), 1.0, 2.0),
        "planetary_vorticity": jnp.clip(jax.random.uniform(seeds[7], (NORTHWARD_CELLS, CIRCUMFERENCE_N), jnp.float32, -1.5, 1.5) * shard_levels(seeds[7], (NORTHWARD_CELLS, CIRCUMFERENCE_N), ((0, 8), (1, 4)), -0.4, 0.0), -1.5, 1.5),
        "scalar_mixing_factor": jnp.clip(jnp.exp(jax.random.uniform(seeds[8], (VERTICAL_LAYERS,), jnp.float32, math.log(0.05), math.log(0.5))), 0.05, 0.5),
        "momentum_mixing_factor": jnp.clip(jnp.exp(jax.random.uniform(seeds[9], (VERTICAL_LAYERS,), jnp.float32, math.log(0.05), math.log(0.5))), 0.05, 0.5),
    }


time_step = 0.2


def tendency(extended, prognostic_quantities, inv_width, inv_height, planetary_vorticity, diffusion):
    cell_mid = prognostic_quantities
    east_side = extended[:, :, 1:-1, 2:]
    west_side = extended[:, :, 1:-1, :-2]
    north_side = extended[:, :, 2:, 1:-1]
    south_side = extended[:, :, :-2, 1:-1]
    grad_east = (east_side - west_side) * 0.5 * inv_width
    grad_north = (north_side - south_side) * 0.5 * inv_height
    laplace = (east_side + west_side - 2.0 * cell_mid) * (inv_width * inv_width) + (north_side + south_side - 2.0 * cell_mid) * (inv_height * inv_height)
    zonal_mid = cell_mid[2]
    north_mid = cell_mid[3]
    advection = -(zonal_mid[None] * grad_east + north_mid[None] * grad_north)
    zeros_plane = jnp.zeros_like(zonal_mid)
    rotation = jnp.stack([zeros_plane, zeros_plane, planetary_vorticity * north_mid, -planetary_vorticity * zonal_mid])
    return advection + diffusion * laplace + rotation


def reference(potential_heat_state, saltiness_anomaly, first_current_component, second_current_component, bathymetry_layer_total, westeast_cell_extent, southnorth_cell_extent, planetary_vorticity, scalar_mixing_factor, momentum_mixing_factor):
    layered_columns = potential_heat_state.shape[0]
    level_index = lax.broadcasted_iota(jnp.int32, (layered_columns,) + bathymetry_layer_total.shape, 0)
    seawater_indicator = (level_index < bathymetry_layer_total[None]).astype(jnp.float32)
    prognostic_quantities = jnp.stack([potential_heat_state, saltiness_anomaly, first_current_component, second_current_component]) * seawater_indicator[None]
    fold_signs = jnp.array([1.0, 1.0, -1.0, -1.0], jnp.float32).reshape(4, 1, 1)
    inv_width = 1.0 / westeast_cell_extent
    inv_height = 1.0 / southnorth_cell_extent
    diffusion = jnp.stack([scalar_mixing_factor, scalar_mixing_factor, momentum_mixing_factor, momentum_mixing_factor])[:, :, None, None]
    for substep in range(STEPS):
        ghost_row = fold_signs * prognostic_quantities[:, :, -1, ::-1]
        bottom_row = jnp.zeros_like(ghost_row)
        padded = jnp.concatenate([bottom_row[:, :, None, :], prognostic_quantities, ghost_row[:, :, None, :]], axis=2)
        extended = jnp.concatenate([padded[..., -1:], padded, padded[..., :1]], axis=3)
        change = tendency(extended, prognostic_quantities, inv_width, inv_height, planetary_vorticity, diffusion)
        prognostic_quantities = prognostic_quantities + time_step * seawater_indicator[None] * change
    return prognostic_quantities[0], prognostic_quantities[1], prognostic_quantities[2], prognostic_quantities[3]
```

```python
import functools

import jax
import jax.numpy as jnp
from jax import lax
from jax.experimental import pallas as pl
from jax.experimental.pallas import tpu as pltpu
from jax.sharding import PartitionSpec as P

STEPS = 3
RIM = 3
time_step = 0.2

MESH = pl.DeviceIdType.MESH


def lanes(shape):
    return lax.broadcasted_iota(jnp.int32, shape, len(shape) - 1)


def exchange(
    x0, x1, x2, x3, bathy, wide, high, vort,
    rows_n, rows_s, strips, strip_n, strip_s,
    out_n, out_s, packed, to_side, from_side, edge_n, edge_s,
    send_sem, recv_sem,
):
    fields = (x0, x1, x2, x3)
    levels, height, width = x0.shape
    lat, lon = lax.axis_index("lat"), lax.axis_index("lon")
    lats, lons = lax.axis_size("lat"), lax.axis_size("lon")
    last = lat == lats - 1
    east = (lat, lax.rem(lon + 1, lons))
    west = (lat, lax.rem(lon + lons - 1, lons))
    north = (
        jnp.where(last, lat, lat + 1),
        jnp.where(last, lons - 1 - lon, lon),
    )
    south = (lat - 1, lon)

    barrier = pltpu.get_barrier_semaphore()
    for peer in (east, west, north):
        pl.semaphore_signal(barrier, inc=1, device_id=peer, device_id_type=MESH)

    @pl.when(lat > 0)
    def _():
        pl.semaphore_signal(barrier, inc=1, device_id=south, device_id_type=MESH)

    lane = lanes((8, width))
    group = lane // 8
    within = lane - group * 8

    @pl.loop(0, height // 8)
    def _(tile):
        rows = pl.ds(pl.multiple_of(tile * 8, 8), 8)
        cols = []
        for f in range(4):
            acc = pltpu.roll(fields[f][0, rows, :], RIM, 1)
            for level in range(1, levels):
                moved = pltpu.roll(fields[f][level, rows, :], (8 * level + RIM) % width, 1)
                acc = jnp.where(group == level, moved, acc)
            packed[f, rows, :] = acc
            cols.append(acc)
        acc = jnp.zeros((8, width), jnp.float32)
        metrics = (bathy[rows, :].astype(jnp.float32), wide[rows, :], high[rows, :], vort[rows, :])
        for m in range(4):
            acc = jnp.where(group == m, pltpu.roll(metrics[m], 8 * m + RIM, 1), acc)
        packed[4, rows, :] = acc
        for pair in range(2):
            one, two = cols[2 * pair], cols[2 * pair + 1]
            to_side[0, pair, rows, :] = jnp.where(within < 4, one, pltpu.roll(two, 4, 1))
            to_side[1, pair, rows, :] = jnp.where(within < 3, pltpu.roll(two, width - 3, 1), one)
        to_side[0, 2, rows, :] = acc
        to_side[1, 2, rows, :] = acc

    @pl.when(lat > 0)
    def _():
        pl.semaphore_wait(barrier, 4)

    @pl.when(lat == 0)
    def _():
        pl.semaphore_wait(barrier, 3)

    def remote(src, dst, which, arrive, peer):
        return pltpu.make_async_remote_copy(
            src_ref=src, dst_ref=dst, send_sem=send_sem.at[which], recv_sem=recv_sem.at[arrive],
            device_id=peer, device_id_type=MESH,
        )

    go_east = remote(to_side.at[0], from_side.at[0], 0, 0, east)
    go_west = remote(to_side.at[1], from_side.at[1], 1, 1, west)
    go_east.start()
    go_west.start()

    for f in range(4):
        for r in range(RIM):
            at = (f * RIM + r) * levels
            out_s[at : at + levels, :] = fields[f][:, r, :]
            out_n[at : at + levels, :] = fields[f][:, height - RIM + r, :]
    base = 4 * RIM * levels
    out_s[base : base + 16, :] = jnp.zeros((16, width), jnp.float32)
    out_n[base : base + 16, :] = jnp.zeros((16, width), jnp.float32)
    for m, metric in enumerate((bathy, wide, high, vort)):
        out_s[base + m * RIM : base + (m + 1) * RIM, :] = metric[0:RIM, :].astype(jnp.float32)
        out_n[base + m * RIM : base + (m + 1) * RIM, :] = metric[height - RIM :, :].astype(jnp.float32)

    def rows_out(to_n, to_s, recv_n, recv_s, first):
        up = remote(to_n, recv_s, first, first, north)
        fold = remote(to_n, recv_n, first, first + 1, north)
        down = remote(to_s, recv_n, first + 1, first + 1, south)

        @pl.when(last)
        def _():
            fold.start()

        @pl.when(lat < lats - 1)
        def _():
            up.start()

        @pl.when(lat > 0)
        def _():
            down.start()

        return up, down

    def rows_in(up, down):
        down.wait_recv()

        @pl.when(lat > 0)
        def _():
            up.wait_recv()

    def rows_sent(up, down):
        up.wait_send()

        @pl.when(lat > 0)
        def _():
            down.wait_send()

    @pl.when(lat == 0)
    def _():
        rows_s[...] = jnp.zeros(rows_s.shape, jnp.float32)
        strip_s[...] = jnp.zeros(strip_s.shape, jnp.float32)

    main = rows_out(out_n, out_s, rows_n, rows_s, 2)

    go_east.wait_recv()
    go_west.wait_recv()

    @pl.loop(0, height // 8)
    def _(tile):
        rows = pl.ds(pl.multiple_of(tile * 8, 8), 8)
        for f in range(5):
            own = packed[f, rows, :]
            got_w = from_side[0, f // 2, rows, :]
            got_e = from_side[1, f // 2, rows, :]
            if f % 2 == 1:
                got_w = pltpu.roll(got_w, width - 4, 1)
                got_e = pltpu.roll(got_e, 3, 1)
            strips[0, f, rows, :] = jnp.where(within < RIM, got_w, own)
            strips[1, f, rows, :] = jnp.where(within < RIM, own, got_e)

    edge_n[30:32, :] = jnp.zeros((2, width), jnp.float32)
    edge_s[30:32, :] = jnp.zeros((2, width), jnp.float32)
    for side in range(2):
        for f in range(5):
            at = (side * 5 + f) * RIM
            edge_s[at : at + RIM, :] = strips[side, f, 0:RIM, :]
            edge_n[at : at + RIM, :] = strips[side, f, height - RIM : height, :]
    ends = rows_out(edge_n, edge_s, strip_n, strip_s, 4)

    go_east.wait_send()
    go_west.wait_send()
    rows_in(*main)
    rows_in(*ends)
    rows_sent(*main)
    rows_sent(*ends)


def substeps(
    tracer_mix, momentum_mix, x0, x1, x2, x3, bathy, wide, high, vort,
    rows_n, rows_s, strips, strip_n, strip_s,
    y0, y1, y2, y3,
    first, second, metric, sides, sides_next, side_metric, link,
):
    fields = (x0, x1, x2, x3)
    outs = (y0, y1, y2, y3)
    levels, height, width = x0.shape
    deep = height + 8
    tiles = deep // 8
    lat = lax.axis_index("lat")
    lats = lax.axis_size("lat")
    last, bottom = lat == lats - 1, lat == 0
    signs = (1.0, 1.0, -1.0, -1.0)
    lane = lanes((8, width))
    row = lax.broadcasted_iota(jnp.int32, (8, width), 0)
    group = lane // 8
    within = lane - group * 8

    def mirrored(value, index):
        pieces = [
            jnp.take_along_axis(value[i : i + 8, :], index, axis=1)
            for i in range(0, value.shape[0], 8)
        ]
        return jnp.concatenate(pieces, axis=0)

    far = rows_n[...]
    flipped = mirrored(far, width - 1 - lane)
    near = rows_s[...]
    side_far = strip_n[...]
    side_flipped = mirrored(side_far, group * 8 + jnp.where(within < 6, 5 - within, within))
    side_near = strip_s[...]

    safe = (0.0, 1.0, 1.0, 0.0)
    base = 4 * RIM * levels
    for m, value in enumerate((bathy, wide, high, vort)):
        metric[m, 0:height, :] = value[...].astype(jnp.float32)
        metric[m, height:deep, :] = jnp.full((8, width), safe[m], jnp.float32)
        for r in range(RIM):
            at = base + m * RIM + r
            fold = base + m * RIM + RIM - 1 - r
            metric[m, height + r : height + r + 1, :] = jnp.where(
                last, flipped[fold : fold + 1, :], far[at : at + 1, :]
            )
            metric[m, deep - RIM + r : deep - RIM + r + 1, :] = jnp.where(
                bottom, safe[m], near[at : at + 1, :]
            )

    for f in range(4):
        for r in range(RIM):
            at = (f * RIM + r) * levels
            fold = (f * RIM + RIM - 1 - r) * levels
            first[f, :, height + r, :] = jnp.where(
                last, signs[f] * flipped[fold : fold + levels, :], far[at : at + levels, :]
            )
            first[f, :, deep - RIM + r, :] = near[at : at + levels, :]

    for side in range(2):
        for f in range(5):
            sides[side, f, 0:height, :] = strips[side, f, :, :]
            if f == 4:
                fill = jnp.where((group == 1) | (group == 2), 1.0, 0.0)
            else:
                fill = jnp.zeros((8, width), jnp.float32)
            sides[side, f, height:deep, :] = fill
            for r in range(RIM):
                at = (side * 5 + f) * RIM + r
                fold = ((1 - side) * 5 + f) * RIM + RIM - 1 - r
                sign = 1.0 if f == 4 else signs[f]
                sides[side, f, height + r : height + r + 1, :] = jnp.where(
                    last, sign * side_flipped[fold : fold + 1, :], side_far[at : at + 1, :]
                )
                got = side_near[at : at + 1, :]
                if f == 4:
                    got = jnp.where(bottom, fill[0:1, :], got)
                sides[side, f, deep - RIM + r : deep - RIM + r + 1, :] = got

    def factors(bath, we, sn, vo):
        a, b = 1.0 / we, 1.0 / sn
        return (
            bath, time_step * a * a, time_step * b * b,
            0.5 * time_step * a, 0.5 * time_step * b, time_step * vo,
        )

    @pl.loop(0, tiles)
    def _(tile):
        rows = pl.ds(pl.multiple_of(tile * 8, 8), 8)
        made = factors(*[metric[m, rows, :] for m in range(4)])
        for m in range(6):
            metric[m, rows, :] = made[m]
        for side in range(2):
            mixed = sides[side, 4, rows, :]
            spread = []
            for m in range(4):
                value = jnp.where(group == m, mixed, 0.0)
                for hop in (8, 16, 32, 64):
                    value = value + pltpu.roll(value, hop, 1)
                spread.append(value)
            made = factors(*spread)
            for m in range(6):
                side_metric[side, m, rows, :] = made[m]
            wet = made[0] > group.astype(jnp.float32)
            for f in range(4):
                sides[side, f, rows, :] = jnp.where(wet, sides[side, f, rows, :], 0.0)

    @pl.loop(0, levels)
    def _(level):
        number = level.astype(jnp.float32)
        for t in range(tiles):
            rows = slice(8 * t, 8 * t + 8)
            wet = metric[0, rows, :] > number
            for f in range(4):
                if t < tiles - 1:
                    value = fields[f][level, rows, :]
                else:
                    value = first[f, level, rows, :]
                    value = jnp.where((row < RIM) | (row >= 8 - RIM), value, 0.0)
                first[f, level, rows, :] = jnp.where(wet, value, 0.0)

    mix_t = jnp.zeros((8, width), jnp.float32)
    mix_m = jnp.zeros((8, width), jnp.float32)
    for level in range(levels):
        mix_t = jnp.where(group == level, tracer_mix[level], mix_t)
        mix_m = jnp.where(group == level, momentum_mix[level], mix_m)

    def advance(read, seam, table, number, mixes, t):
        centre = [read(f, 8 * t, 8) for f in range(4)]

        def north_of(f):
            if t < tiles - 1:
                return read(f, 8 * t + 1, 8)
            wrapped = pltpu.roll(read(f, 0, 8), 7, 0)
            return jnp.where(row == 7, wrapped, pltpu.roll(centre[f], 7, 0))

        def south_of(f):
            if t > 0:
                return read(f, 8 * t - 1, 8)
            wrapped = pltpu.roll(read(f, deep - 8, 8), 1, 0)
            return jnp.where(row == 0, wrapped, pltpu.roll(centre[f], 1, 0))

        bath, a2, b2, ah, bh, vo = [table(m, 8 * t) for m in range(6)]
        wet = bath > number
        a2 = jnp.where(wet, a2, 0.0)
        b2 = jnp.where(wet, b2, 0.0)
        u, v = centre[2], centre[3]
        du, dv = u * ah, v * bh
        results = []
        for f in range(4):
            if f % 2 == 0:
                da, db = mixes[f // 2] * a2, mixes[f // 2] * b2
                ce, cw, cn, cs = da - du, da + du, db - dv, db + dv
                cc = 1.0 - 2.0 * (da + db)
            c = centre[f]
            if seam is None:
                e, w = pltpu.roll(c, width - 1, 1), pltpu.roll(c, 1, 1)
            else:
                z = seam(f, t)
                e = pltpu.roll(jnp.where(lane == 0, z, c), width - 1, 1)
                w = pltpu.roll(jnp.where(lane == width - 1, z, c), 1, 1)
            new = cc * c + (ce * e + cw * w) + (cn * north_of(f) + cs * south_of(f))
            if f == 2:
                new = new + vo * v
            if f == 3:
                new = new - vo * u
            results.append(new)
        return results

    def main_step(source, store, count):
        @pl.loop(0, levels)
        def _(level):
            number = level.astype(jnp.float32)
            mixes = (tracer_mix[level], momentum_mix[level])
            for t in range(count):
                new = advance(
                    lambda f, start, size: source[f, level, start : start + size, :],
                    lambda f, t: pltpu.roll(link[f, 8 * t : 8 * t + 8, :], width - 3 - 8 * level, 1),
                    lambda m, start: metric[m, start : start + 8, :],
                    number, mixes, t,
                )
                for f in range(4):
                    store(f, level, t, new[f])

    def side_step(source, target):
        for side in range(2):
            for t in range(tiles):
                new = advance(
                    lambda f, start, size: source[side, f, start : start + size, :],
                    None,
                    lambda m, start: side_metric[side, m, start : start + 8, :],
                    group.astype(jnp.float32), (mix_t, mix_m), t,
                )
                for f in range(4):
                    target[side, f, 8 * t : 8 * t + 8, :] = new[f]

    def join(source):
        for f in range(4):
            for t in range(tiles):
                rows = slice(8 * t, 8 * t + 8)
                link[f, rows, :] = jnp.where(within == 2, source[0, f, rows, :], source[1, f, rows, :])

    def into(buffer):
        def store(f, level, t, value):
            buffer[f, level, 8 * t : 8 * t + 8, :] = value
        return store

    def final(f, level, t, value):
        outs[f][level, 8 * t : 8 * t + 8, :] = value

    state, spare = first, second
    side_state, side_spare = sides, sides_next
    for step in range(STEPS):
        join(side_state)
        if step < STEPS - 1:
            main_step(state, into(spare), tiles)
            side_step(side_state, side_spare)
        else:
            main_step(state, final, tiles - 1)
        state, spare = spare, state
        side_state, side_spare = side_spare, side_state


def on_device(
    potential_heat_state,
    saltiness_anomaly,
    first_current_component,
    second_current_component,
    bathymetry_layer_total,
    westeast_cell_extent,
    southnorth_cell_extent,
    planetary_vorticity,
    scalar_mixing_factor,
    momentum_mixing_factor,
):
    fields = (potential_heat_state, saltiness_anomaly, first_current_component, second_current_component)
    metrics = (bathymetry_layer_total, westeast_cell_extent, southnorth_cell_extent, planetary_vorticity)
    levels, height, width = potential_heat_state.shape
    f32 = jnp.float32
    message = 4 * RIM * levels + 16
    deep = height + 8
    vmem = pl.BlockSpec(memory_space=pltpu.VMEM)
    smem = pl.BlockSpec(memory_space=pltpu.SMEM)
    rims = pl.pallas_call(
        exchange,
        out_shape=(
            jax.ShapeDtypeStruct((message, width), f32),
            jax.ShapeDtypeStruct((message, width), f32),
            jax.ShapeDtypeStruct((2, 5, height, width), f32),
            jax.ShapeDtypeStruct((32, width), f32),
            jax.ShapeDtypeStruct((32, width), f32),
        ),
        in_specs=[vmem] * 8,
        out_specs=[vmem] * 5,
        scratch_shapes=[
            pltpu.VMEM((message, width), f32),
            pltpu.VMEM((message, width), f32),
            pltpu.VMEM((5, height, width), f32),
            pltpu.VMEM((2, 3, height, width), f32),
            pltpu.VMEM((2, 3, height, width), f32),
            pltpu.VMEM((32, width), f32),
            pltpu.VMEM((32, width), f32),
            pltpu.SemaphoreType.DMA((6,)),
            pltpu.SemaphoreType.DMA((6,)),
        ],
        compiler_params=pltpu.CompilerParams(
            collective_id=0, has_side_effects=True, vmem_limit_bytes=16 * 2**20
        ),
        name="exchange",
    )(*fields, *metrics)
    whole = jax.ShapeDtypeStruct((levels, height, width), f32)
    return pl.pallas_call(
        substeps,
        out_shape=(whole,) * 4,
        in_specs=[smem] * 2 + [vmem] * 13,
        out_specs=[vmem] * 4,
        scratch_shapes=[
            pltpu.VMEM((4, levels, deep, width), f32),
            pltpu.VMEM((4, levels, deep, width), f32),
            pltpu.VMEM((6, deep, width), f32),
            pltpu.VMEM((2, 5, deep, width), f32),
            pltpu.VMEM((2, 5, deep, width), f32),
            pltpu.VMEM((2, 6, deep, width), f32),
            pltpu.VMEM((4, deep, width), f32),
        ],
        compiler_params=pltpu.CompilerParams(vmem_limit_bytes=24 * 2**20),
        name="substeps",
    )(scalar_mixing_factor, momentum_mixing_factor, *fields, *metrics, *rims)


def solution(mesh):
    state, plane = P(None, "lat", "lon"), P("lat", "lon")
    return jax.shard_map(
        on_device,
        mesh=mesh,
        in_specs=(state,) * 4 + (plane,) * 4 + (P(), P()),
        out_specs=(state,) * 4,
        check_vma=False,
    )
```

```python
import functools

import jax
import jax.numpy as jnp
from jax import lax
from jax.experimental import pallas as pl
from jax.experimental.pallas import tpu as pltpu
from jax.sharding import PartitionSpec as P

STEPS = 3
RIM = 3
time_step = 0.2

MESH = pl.DeviceIdType.MESH


def lanes(shape):
    return lax.broadcasted_iota(jnp.int32, shape, len(shape) - 1)


def factors(bath, we, sn, vo):
    a, b = 1.0 / we, 1.0 / sn
    return (
        bath, time_step * a * a, time_step * b * b,
        0.5 * time_step * a, 0.5 * time_step * b, time_step * vo,
    )


def exchange(
    x0, x1, x2, x3, bathy, wide, high, vort,
    state, table, sides, side_metric,
    field, whole, bath, metric,
    rows_n, rows_s, strips, strip_n, strip_s,
    out_n, out_s, packed, to_side, from_side, edge_n, edge_s,
    send_sem, recv_sem, load_sem,
):
    levels, width = state.shape[2], state.shape[3]
    height = wide.shape[0]
    deep = height + 8
    lat, lon = lax.axis_index("lat"), lax.axis_index("lon")
    lats, lons = lax.axis_size("lat"), lax.axis_size("lon")
    last, bottom = lat == lats - 1, lat == 0
    east = (lat, lax.rem(lon + 1, lons))
    west = (lat, lax.rem(lon + lons - 1, lons))
    north = (
        jnp.where(last, lat, lat + 1),
        jnp.where(last, lons - 1 - lon, lon),
    )
    south = (lat - 1, lon)

    loads = [
        pltpu.make_async_copy(x, field.at[f], load_sem.at[f]) for f, x in enumerate((x0, x1, x2, x3))
    ]
    loads.append(pltpu.make_async_copy(bathy, bath, load_sem.at[4]))
    loads += [
        pltpu.make_async_copy(x, whole.at[m], load_sem.at[5 + m]) for m, x in enumerate((wide, high, vort))
    ]
    for load in loads:
        load.start()

    barrier = pltpu.get_barrier_semaphore()
    for peer in (east, west, north):
        pl.semaphore_signal(barrier, inc=1, device_id=peer, device_id_type=MESH)

    @pl.when(lat > 0)
    def _():
        pl.semaphore_signal(barrier, inc=1, device_id=south, device_id_type=MESH)

    lane = lanes((8, width))
    row = lax.broadcasted_iota(jnp.int32, (8, width), 0)
    group = lane // 8
    within = lane - group * 8
    for load in loads:
        load.wait()

    @pl.loop(0, height // 8)
    def _(tile):
        start = pl.multiple_of(tile * 8, 8)
        rows = pl.ds(start, 8)
        cols = []
        for f in range(4):
            acc = pltpu.roll(field[f, rows, :], 8 * (levels - 1) + RIM, 1)
            for level in range(1, levels):
                spot = levels - 1 - level
                at = pl.ds(pl.multiple_of(start + level * height, 8), 8)
                acc = jnp.where(group == spot, pltpu.roll(field[f, at, :], 8 * spot + RIM, 1), acc)
            packed[f, rows, :] = acc
            cols.append(acc)
        acc = jnp.zeros((8, width), jnp.float32)
        raw = (bath[rows, :].astype(jnp.float32), whole[0, rows, :], whole[1, rows, :], whole[2, rows, :])
        for m in range(4):
            metric[m, rows, :] = raw[m]
            acc = jnp.where(group == m, pltpu.roll(raw[m], 8 * m + RIM, 1), acc)
        packed[4, rows, :] = acc
        for pair in range(2):
            one, two = cols[2 * pair], cols[2 * pair + 1]
            to_side[0, pair, rows, :] = jnp.where(within < 4, one, pltpu.roll(two, 4, 1))
            to_side[1, pair, rows, :] = jnp.where(within < 3, pltpu.roll(two, width - 3, 1), one)
        to_side[0, 2, rows, :] = acc
        to_side[1, 2, rows, :] = acc

    @pl.when(lat > 0)
    def _():
        pl.semaphore_wait(barrier, 4)

    @pl.when(lat == 0)
    def _():
        pl.semaphore_wait(barrier, 3)

    def remote(src, dst, which, arrive, peer):
        return pltpu.make_async_remote_copy(
            src_ref=src, dst_ref=dst, send_sem=send_sem.at[which], recv_sem=recv_sem.at[arrive],
            device_id=peer, device_id_type=MESH,
        )

    go_east = remote(to_side.at[0], from_side.at[0], 0, 0, east)
    go_west = remote(to_side.at[1], from_side.at[1], 1, 1, west)
    go_east.start()
    go_west.start()

    def column(f, r, half):
        return field[f, pl.ds(r + half * 8 * height, 8, stride=height), :]

    for f in range(4):
        for r in range(RIM):
            at = (f * RIM + r) * levels
            for half in range(levels // 8):
                rows = slice(at + 8 * half, at + 8 * half + 8)
                out_s[rows, :] = column(f, r, half)
                out_n[rows, :] = column(f, height - RIM + r, half)
    base = 4 * RIM * levels
    out_s[base : base + 16, :] = jnp.zeros((16, width), jnp.float32)
    out_n[base : base + 16, :] = jnp.zeros((16, width), jnp.float32)
    for m in range(4):
        out_s[base + m * RIM : base + (m + 1) * RIM, :] = metric[m, 0:RIM, :]
        out_n[base + m * RIM : base + (m + 1) * RIM, :] = metric[m, height - RIM : height, :]

    def rows_out(to_n, to_s, recv_n, recv_s, first):
        up = remote(to_n, recv_s, first, first, north)
        fold = remote(to_n, recv_n, first, first + 1, north)
        down = remote(to_s, recv_n, first + 1, first + 1, south)

        @pl.when(last)
        def _():
            fold.start()

        @pl.when(lat < lats - 1)
        def _():
            up.start()

        @pl.when(lat > 0)
        def _():
            down.start()

        return up, down

    def rows_in(up, down):
        down.wait_recv()

        @pl.when(lat > 0)
        def _():
            up.wait_recv()

    def rows_sent(up, down):
        up.wait_send()

        @pl.when(lat > 0)
        def _():
            down.wait_send()

    @pl.when(lat == 0)
    def _():
        rows_s[...] = jnp.zeros(rows_s.shape, jnp.float32)
        strip_s[...] = jnp.zeros(strip_s.shape, jnp.float32)

    main = rows_out(out_n, out_s, rows_n, rows_s, 2)

    @pl.loop(0, height // 8)
    def _(tile):
        rows = pl.ds(pl.multiple_of(tile * 8, 8), 8)
        made = factors(*[metric[m, rows, :] for m in range(4)])
        for m in range(6):
            for i in range(8):
                table[m, RIM + tile * 8 + i, :, :] = jnp.broadcast_to(made[m][i : i + 1, :], (8, width))

    def wet_of(at, half):
        return table[0, at, :, :] > (row + 8 * half).astype(jnp.float32)

    @pl.loop(0, height, unroll=2)
    def _(r):
        for half in range(levels // 8):
            wet = wet_of(RIM + r, half)
            for f in range(4):
                state[f, RIM + r, 8 * half : 8 * half + 8, :] = jnp.where(wet, column(f, r, half), 0.0)

    go_east.wait_recv()
    go_west.wait_recv()

    @pl.loop(0, height // 8)
    def _(tile):
        rows = pl.ds(pl.multiple_of(tile * 8, 8), 8)
        for f in range(5):
            own = packed[f, rows, :]
            got_w = from_side[0, f // 2, rows, :]
            got_e = from_side[1, f // 2, rows, :]
            if f % 2 == 1:
                got_w = pltpu.roll(got_w, width - 4, 1)
                got_e = pltpu.roll(got_e, 3, 1)
            strips[0, f, rows, :] = jnp.where(within < RIM, got_w, own)
            strips[1, f, rows, :] = jnp.where(within < RIM, own, got_e)

    edge_n[30:32, :] = jnp.zeros((2, width), jnp.float32)
    edge_s[30:32, :] = jnp.zeros((2, width), jnp.float32)
    for side in range(2):
        for f in range(5):
            at = (side * 5 + f) * RIM
            edge_s[at : at + RIM, :] = strips[side, f, 0:RIM, :]
            edge_n[at : at + RIM, :] = strips[side, f, height - RIM : height, :]
    ends = rows_out(edge_n, edge_s, strip_n, strip_s, 4)

    def side_tables(rows):
        for side in range(2):
            mixed = strips[side, 4, rows, :]
            spread = []
            for m in range(4):
                value = jnp.where(group == m, mixed, 0.0)
                for hop in (8, 16, 32, 64):
                    value = value + pltpu.roll(value, hop, 1)
                spread.append(value)
            made = factors(*spread)
            for m in range(6):
                side_metric[side, m, rows, :] = made[m]
            wet = made[0] > (levels - 1 - group).astype(jnp.float32)
            for f in range(4):
                sides[side, f, rows, :] = jnp.where(wet, strips[side, f, rows, :], 0.0)

    @pl.loop(0, height // 8)
    def _(tile):
        side_tables(pl.ds(pl.multiple_of(tile * 8, 8), 8))

    go_east.wait_send()
    go_west.wait_send()
    rows_in(*main)

    def mirrored(value, index):
        pieces = [
            jnp.take_along_axis(value[i : i + 8, :], index, axis=1)
            for i in range(0, value.shape[0], 8)
        ]
        return jnp.concatenate(pieces, axis=0)

    signs = (1.0, 1.0, -1.0, -1.0)
    safe = (0.0, 1.0, 1.0, 0.0)
    turn = width - 1 - lane
    far, near = rows_n[base : base + 16, :], rows_s[base : base + 16, :]
    flipped = mirrored(far, turn)
    for k in range(RIM):
        up = [
            jnp.where(
                last,
                flipped[m * RIM + RIM - 1 - k : m * RIM + RIM - k, :],
                far[m * RIM + k : m * RIM + k + 1, :],
            )
            for m in range(4)
        ]
        down = [
            jnp.where(bottom, safe[m], near[m * RIM + k : m * RIM + k + 1, :]) for m in range(4)
        ]
        for at, raw in ((RIM + height + k, up), (k, down)):
            made = factors(*raw)
            for m in range(6):
                table[m, at, :, :] = jnp.broadcast_to(made[m], (8, width))
        for half in range(levels // 8):
            wet_up, wet_down = wet_of(RIM + height + k, half), wet_of(k, half)
            for f in range(4):
                span = slice(8 * half, 8 * half + 8)
                at = (f * RIM + k) * levels + 8 * half
                fold = (f * RIM + RIM - 1 - k) * levels + 8 * half
                turned = signs[f] * jnp.take_along_axis(rows_n[fold : fold + 8, :], turn, axis=1)
                value = jnp.where(last, turned, rows_n[at : at + 8, :])
                state[f, RIM + height + k, span, :] = jnp.where(wet_up, value, 0.0)
                state[f, k, span, :] = jnp.where(wet_down, rows_s[at : at + 8, :], 0.0)

    rows_in(*ends)
    side_far = strip_n[...]
    side_flipped = mirrored(side_far, group * 8 + jnp.where(within < 6, 5 - within, within))
    side_near = strip_s[...]
    for side in range(2):
        for f in range(5):
            if f == 4:
                fill = jnp.where((group == 1) | (group == 2), 1.0, 0.0)
            else:
                fill = jnp.zeros((8, width), jnp.float32)
            strips[side, f, height:deep, :] = fill
            for r in range(RIM):
                at = (side * 5 + f) * RIM + r
                fold = ((1 - side) * 5 + f) * RIM + RIM - 1 - r
                sign = 1.0 if f == 4 else signs[f]
                strips[side, f, height + r : height + r + 1, :] = jnp.where(
                    last, sign * side_flipped[fold : fold + 1, :], side_far[at : at + 1, :]
                )
                got = side_near[at : at + 1, :]
                if f == 4:
                    got = jnp.where(bottom, fill[0:1, :], got)
                strips[side, f, deep - RIM + r : deep - RIM + r + 1, :] = got
    side_tables(slice(height, deep))
    rows_sent(*main)
    rows_sent(*ends)


def substeps(
    tracer_mix, momentum_mix, state, table, sides, side_metric,
    y0, y1, y2, y3,
    second, third, result, sides_second, sides_third, link, store_sem,
):
    outs = (y0, y1, y2, y3)
    rows_deep, levels, width = state.shape[1:]
    height = rows_deep - 2 * RIM
    halves = levels // 8
    tiles = sides.shape[2] // 8
    lane = lanes((8, width))
    row = lax.broadcasted_iota(jnp.int32, (8, width), 0)
    group = lane // 8
    within = lane - group * 8

    def levelled(mix, half):
        value = jnp.zeros((8, width), jnp.float32)
        for i in range(8):
            value = jnp.where(row == i, mix[8 * half + i], value)
        return value

    def grouped(mix):
        value = jnp.zeros((8, width), jnp.float32)
        for level in range(levels):
            value = jnp.where(group == levels - 1 - level, mix[level], value)
        return value

    mixes = [(levelled(tracer_mix, h), levelled(momentum_mix, h)) for h in range(halves)]
    numbers = [(row + 8 * h).astype(jnp.float32) for h in range(halves)]

    def update(centre, easts, wests, norths, souths, factor, number, mix):
        bath, a2, b2, ah, bh, vo = factor
        wet = bath > number
        a2 = jnp.where(wet, a2, 0.0)
        b2 = jnp.where(wet, b2, 0.0)
        u, v = centre[2], centre[3]
        du, dv = u * ah, v * bh
        results = []
        for f in range(4):
            if f % 2 == 0:
                da, db = mix[f // 2] * a2, mix[f // 2] * b2
                ce, cw, cn, cs = da - du, da + du, db - dv, db + dv
                cc = 1.0 - 2.0 * (da + db)
            new = cc * centre[f] + (ce * easts[f] + cw * wests[f])
            new = new + (cn * norths[f] + cs * souths[f])
            if f == 2:
                new = new + vo * v
            if f == 3:
                new = new - vo * u
            results.append(new)
        return results

    def main_step(source, store, low, high):
        @pl.loop(low, high, unroll=2)
        def _(r):
            factor = [table[m, r, :, :] for m in range(6)]
            seam_row = lax.rem(r + 8 * tiles - RIM, 8 * tiles)
            seams = [
                jnp.broadcast_to(link[f, pl.ds(seam_row, 1), :], (8, width)) for f in range(4)
            ]
            for half in range(halves):
                span = slice(8 * half, 8 * half + 8)
                centre = [source[f, r, span, :] for f in range(4)]
                easts, wests = [], []
                for f in range(4):
                    z = pltpu.roll(seams[f], width - 3 - 8 * (levels - 1) + 64 * half, 1, stride=8, stride_axis=0)
                    easts.append(pltpu.roll(jnp.where(lane == 0, z, centre[f]), width - 1, 1))
                    wests.append(pltpu.roll(jnp.where(lane == width - 1, z, centre[f]), 1, 1))
                norths = [source[f, r + 1, span, :] for f in range(4)]
                souths = [source[f, r - 1, span, :] for f in range(4)]
                new = update(centre, easts, wests, norths, souths, factor, numbers[half], mixes[half])
                for f in range(4):
                    store(f, r, half, new[f])

    def side_step(source, target):
        mix = (grouped(tracer_mix), grouped(momentum_mix))
        number = (levels - 1 - group).astype(jnp.float32)
        for side in range(2):
            for t in range(tiles):
                rows = slice(8 * t, 8 * t + 8)
                prior, following = (t + tiles - 1) % tiles * 8, (t + 1) % tiles * 8
                centre = [source[side, f, rows, :] for f in range(4)]
                easts = [pltpu.roll(c, width - 1, 1) for c in centre]
                wests = [pltpu.roll(c, 1, 1) for c in centre]
                norths = [
                    jnp.where(
                        row == 7,
                        pltpu.roll(source[side, f, following : following + 8, :], 7, 0),
                        pltpu.roll(centre[f], 7, 0),
                    )
                    for f in range(4)
                ]
                souths = [
                    jnp.where(
                        row == 0,
                        pltpu.roll(source[side, f, prior : prior + 8, :], 1, 0),
                        pltpu.roll(centre[f], 1, 0),
                    )
                    for f in range(4)
                ]
                factor = [side_metric[side, m, rows, :] for m in range(6)]
                new = update(centre, easts, wests, norths, souths, factor, number, mix)
                for f in range(4):
                    target[side, f, rows, :] = new[f]

    def join(source):
        for f in range(4):
            for t in range(tiles):
                rows = slice(8 * t, 8 * t + 8)
                link[f, rows, :] = jnp.where(within == 2, source[0, f, rows, :], source[1, f, rows, :])

    def into(buffer):
        def store(f, r, half, value):
            buffer[f, r, 8 * half : 8 * half + 8, :] = value
        return store

    def final(f, r, half, value):
        result[f, pl.ds(r - RIM + half * 8 * height, 8, stride=height), :] = value

    join(sides)
    main_step(state, into(second), 1, rows_deep - 1)
    side_step(sides, sides_second)
    join(sides_second)
    main_step(second, into(third), 2, rows_deep - 2)
    side_step(sides_second, sides_third)
    join(sides_third)
    main_step(third, final, 3, rows_deep - 3)
    stores = [
        pltpu.make_async_copy(result.at[f], outs[f], store_sem.at[f]) for f in range(4)
    ]
    for copy in stores:
        copy.start()
    for copy in stores:
        copy.wait()


def on_device(
    potential_heat_state,
    saltiness_anomaly,
    first_current_component,
    second_current_component,
    bathymetry_layer_total,
    westeast_cell_extent,
    southnorth_cell_extent,
    planetary_vorticity,
    scalar_mixing_factor,
    momentum_mixing_factor,
):
    fields = (potential_heat_state, saltiness_anomaly, first_current_component, second_current_component)
    metrics = (bathymetry_layer_total, westeast_cell_extent, southnorth_cell_extent, planetary_vorticity)
    levels, height, width = potential_heat_state.shape
    f32 = jnp.float32
    message = 4 * RIM * levels + 16
    deep = height + 8
    flat = (levels * height, width)
    vmem = pl.BlockSpec(memory_space=pltpu.VMEM)
    smem = pl.BlockSpec(memory_space=pltpu.SMEM)
    anywhere = pl.BlockSpec(memory_space=pltpu.HBM)
    laid = pl.pallas_call(
        exchange,
        out_shape=(
            pltpu.VMEM((4, height + 2 * RIM, levels, width), f32),
            pltpu.VMEM((6, height + 2 * RIM, 8, width), f32),
            pltpu.VMEM((2, 4, deep, width), f32),
            pltpu.VMEM((2, 6, deep, width), f32),
        ),
        in_specs=[anywhere] * 8,
        out_specs=[vmem] * 4,
        scratch_shapes=[
            pltpu.VMEM((4,) + flat, f32),
            pltpu.VMEM((3, height, width), f32),
            pltpu.VMEM((height, width), jnp.int32),
            pltpu.VMEM((4, height, width), f32),
            pltpu.VMEM((message, width), f32),
            pltpu.VMEM((message, width), f32),
            pltpu.VMEM((2, 5, deep, width), f32),
            pltpu.VMEM((32, width), f32),
            pltpu.VMEM((32, width), f32),
            pltpu.VMEM((message, width), f32),
            pltpu.VMEM((message, width), f32),
            pltpu.VMEM((5, height, width), f32),
            pltpu.VMEM((2, 3, height, width), f32),
            pltpu.VMEM((2, 3, height, width), f32),
            pltpu.VMEM((32, width), f32),
            pltpu.VMEM((32, width), f32),
            pltpu.SemaphoreType.DMA((6,)),
            pltpu.SemaphoreType.DMA((6,)),
            pltpu.SemaphoreType.DMA((8,)),
        ],
        compiler_params=pltpu.CompilerParams(
            collective_id=0, has_side_effects=True, vmem_limit_bytes=int(59.4 * 2**20)
        ),
        name="exchange",
    )(*[x.reshape(flat) for x in fields], *metrics)
    news = pl.pallas_call(
        substeps,
        out_shape=(jax.ShapeDtypeStruct(flat, f32),) * 4,
        in_specs=[smem] * 2 + [vmem] * 4,
        out_specs=[anywhere] * 4,
        scratch_shapes=[
            pltpu.VMEM((4, height + 2 * RIM, levels, width), f32),
            pltpu.VMEM((4, height + 2 * RIM, levels, width), f32),
            pltpu.VMEM((4,) + flat, f32),
            pltpu.VMEM((2, 4, deep, width), f32),
            pltpu.VMEM((2, 4, deep, width), f32),
            pltpu.VMEM((4, deep, width), f32),
            pltpu.SemaphoreType.DMA((4,)),
        ],
        compiler_params=pltpu.CompilerParams(vmem_limit_bytes=24 * 2**20),
        name="substeps",
    )(scalar_mixing_factor, momentum_mixing_factor, *laid)
    return tuple(x.reshape((levels, height, width)) for x in news)


def solution(mesh):
    state, plane = P(None, "lat", "lon"), P("lat", "lon")
    return jax.shard_map(
        on_device,
        mesh=mesh,
        in_specs=(state,) * 4 + (plane,) * 4 + (P(), P()),
        out_specs=(state,) * 4,
        check_vma=False,
    )
```

```python
import functools

import jax
import jax.numpy as jnp
from jax import lax
from jax.experimental import pallas as pl
from jax.experimental.pallas import tpu as pltpu
from jax.sharding import PartitionSpec as P

STEPS = 3
RIM = 3
time_step = 0.2

MESH = pl.DeviceIdType.MESH


def lanes(shape):
    return lax.broadcasted_iota(jnp.int32, shape, len(shape) - 1)


def factors(bath, we, sn, vo):
    a, b = 1.0 / we, 1.0 / sn
    return (
        bath, time_step * a * a, time_step * b * b,
        0.5 * time_step * a, 0.5 * time_step * b, time_step * vo,
    )


def exchange(
    x0, x1, x2, x3, bathy, wide, high, vort, tracer_mix, momentum_mix,
    state, table, sides, side_metric, mixing,
    factor_t, factor_m, field, whole, bath, metric,
    rows_n, rows_s, strips, strip_n, strip_s,
    out_n, out_s, packed, to_side, from_side, edge_n, edge_s,
    send_sem, recv_sem, load_sem,
):
    levels, width = state.shape[2], state.shape[3]
    height = wide.shape[0]
    deep = height + 8
    lat, lon = lax.axis_index("lat"), lax.axis_index("lon")
    lats, lons = lax.axis_size("lat"), lax.axis_size("lon")
    last, bottom = lat == lats - 1, lat == 0
    east = (lat, lax.rem(lon + 1, lons))
    west = (lat, lax.rem(lon + lons - 1, lons))
    north = (
        jnp.where(last, lat, lat + 1),
        jnp.where(last, lons - 1 - lon, lon),
    )
    south = (lat - 1, lon)

    loads = [
        pltpu.make_async_copy(x, field.at[f], load_sem.at[f]) for f, x in enumerate((x0, x1, x2, x3))
    ]
    loads.append(pltpu.make_async_copy(bathy, bath, load_sem.at[4]))
    loads += [
        pltpu.make_async_copy(x, whole.at[m], load_sem.at[5 + m]) for m, x in enumerate((wide, high, vort))
    ]
    loads += [
        pltpu.make_async_copy(tracer_mix, factor_t, load_sem.at[8]),
        pltpu.make_async_copy(momentum_mix, factor_m, load_sem.at[9]),
    ]
    for load in loads:
        load.start()

    barrier = pltpu.get_barrier_semaphore()
    for peer in (east, west, north):
        pl.semaphore_signal(barrier, inc=1, device_id=peer, device_id_type=MESH)

    @pl.when(lat > 0)
    def _():
        pl.semaphore_signal(barrier, inc=1, device_id=south, device_id_type=MESH)

    lane = lanes((8, width))
    row = lax.broadcasted_iota(jnp.int32, (8, width), 0)
    group = lane // 8
    within = lane - group * 8
    for load in loads:
        load.wait()

    @pl.loop(0, height // 8)
    def _(tile):
        start = pl.multiple_of(tile * 8, 8)
        rows = pl.ds(start, 8)
        cols = []
        for f in range(4):
            acc = pltpu.roll(field[f, rows, :], 8 * (levels - 1) + RIM, 1)
            for level in range(1, levels):
                spot = levels - 1 - level
                at = pl.ds(pl.multiple_of(start + level * height, 8), 8)
                acc = jnp.where(group == spot, pltpu.roll(field[f, at, :], 8 * spot + RIM, 1), acc)
            packed[f, rows, :] = acc
            cols.append(acc)
        acc = jnp.zeros((8, width), jnp.float32)
        raw = (bath[rows, :].astype(jnp.float32), whole[0, rows, :], whole[1, rows, :], whole[2, rows, :])
        for m in range(4):
            metric[m, rows, :] = raw[m]
            acc = jnp.where(group == m, pltpu.roll(raw[m], 8 * m + RIM, 1), acc)
        packed[4, rows, :] = acc
        for pair in range(2):
            one, two = cols[2 * pair], cols[2 * pair + 1]
            to_side[0, pair, rows, :] = jnp.where(within < 4, one, pltpu.roll(two, 4, 1))
            to_side[1, pair, rows, :] = jnp.where(within < 3, pltpu.roll(two, width - 3, 1), one)
        to_side[0, 2, rows, :] = acc
        to_side[1, 2, rows, :] = acc

    @pl.when(lat > 0)
    def _():
        pl.semaphore_wait(barrier, 4)

    @pl.when(lat == 0)
    def _():
        pl.semaphore_wait(barrier, 3)

    def remote(src, dst, which, arrive, peer):
        return pltpu.make_async_remote_copy(
            src_ref=src, dst_ref=dst, send_sem=send_sem.at[which], recv_sem=recv_sem.at[arrive],
            device_id=peer, device_id_type=MESH,
        )

    go_east = remote(to_side.at[0], from_side.at[0], 0, 0, east)
    go_west = remote(to_side.at[1], from_side.at[1], 1, 1, west)
    go_east.start()
    go_west.start()

    def column(f, r, half):
        return field[f, pl.ds(r + half * 8 * height, 8, stride=height), :]

    for f in range(4):
        for r in range(RIM):
            at = (f * RIM + r) * levels
            for half in range(levels // 8):
                rows = slice(at + 8 * half, at + 8 * half + 8)
                out_s[rows, :] = column(f, r, half)
                out_n[rows, :] = column(f, height - RIM + r, half)
    base = 4 * RIM * levels
    out_s[base : base + 16, :] = jnp.zeros((16, width), jnp.float32)
    out_n[base : base + 16, :] = jnp.zeros((16, width), jnp.float32)
    for m in range(4):
        out_s[base + m * RIM : base + (m + 1) * RIM, :] = metric[m, 0:RIM, :]
        out_n[base + m * RIM : base + (m + 1) * RIM, :] = metric[m, height - RIM : height, :]

    def rows_out(to_n, to_s, recv_n, recv_s, first):
        up = remote(to_n, recv_s, first, first, north)
        fold = remote(to_n, recv_n, first, first + 1, north)
        down = remote(to_s, recv_n, first + 1, first + 1, south)

        @pl.when(last)
        def _():
            fold.start()

        @pl.when(lat < lats - 1)
        def _():
            up.start()

        @pl.when(lat > 0)
        def _():
            down.start()

        return up, down

    def rows_in(up, down):
        down.wait_recv()

        @pl.when(lat > 0)
        def _():
            up.wait_recv()

    def rows_sent(up, down):
        up.wait_send()

        @pl.when(lat > 0)
        def _():
            down.wait_send()

    @pl.when(lat == 0)
    def _():
        rows_s[...] = jnp.zeros(rows_s.shape, jnp.float32)
        strip_s[...] = jnp.zeros(strip_s.shape, jnp.float32)

    main = rows_out(out_n, out_s, rows_n, rows_s, 2)

    @pl.loop(0, height // 8)
    def _(tile):
        rows = pl.ds(pl.multiple_of(tile * 8, 8), 8)
        made = factors(*[metric[m, rows, :] for m in range(4)])
        for m in range(6):
            for i in range(8):
                table[m, RIM + tile * 8 + i, :, :] = jnp.broadcast_to(made[m][i : i + 1, :], (8, width))

    def wet_of(at, half):
        return table[0, at, :, :] > (row + 8 * half).astype(jnp.float32)

    go_east.wait_recv()
    go_west.wait_recv()

    @pl.loop(0, height // 8)
    def _(tile):
        rows = pl.ds(pl.multiple_of(tile * 8, 8), 8)
        for f in range(5):
            own = packed[f, rows, :]
            got_w = from_side[0, f // 2, rows, :]
            got_e = from_side[1, f // 2, rows, :]
            if f % 2 == 1:
                got_w = pltpu.roll(got_w, width - 4, 1)
                got_e = pltpu.roll(got_e, 3, 1)
            strips[0, f, rows, :] = jnp.where(within < RIM, got_w, own)
            strips[1, f, rows, :] = jnp.where(within < RIM, own, got_e)

    edge_n[30:32, :] = jnp.zeros((2, width), jnp.float32)
    edge_s[30:32, :] = jnp.zeros((2, width), jnp.float32)
    for side in range(2):
        for f in range(5):
            at = (side * 5 + f) * RIM
            edge_s[at : at + RIM, :] = strips[side, f, 0:RIM, :]
            edge_n[at : at + RIM, :] = strips[side, f, height - RIM : height, :]
    ends = rows_out(edge_n, edge_s, strip_n, strip_s, 4)

    @pl.loop(0, height, unroll=8)
    def _(r):
        for half in range(levels // 8):
            wet = wet_of(RIM + r, half)
            for f in range(4):
                state[f, RIM + r, 8 * half : 8 * half + 8, :] = jnp.where(wet, column(f, r, half), 0.0)

    for k, mix in enumerate((factor_t, factor_m)):
        spread = jnp.zeros((8, width), jnp.float32)
        for half in range(levels // 8):
            value = jnp.zeros((8, width), jnp.float32)
            for i in range(8):
                value = jnp.where(row == i, mix[8 * half + i], value)
                spread = jnp.where(group == levels - 1 - 8 * half - i, mix[8 * half + i], spread)
            mixing[(levels // 8 + 1) * k + half] = value
        mixing[(levels // 8 + 1) * k + levels // 8] = spread

    def side_tables(rows):
        for side in range(2):
            mixed = strips[side, 4, rows, :]
            spread = []
            for m in range(4):
                value = jnp.where(group == m, mixed, 0.0)
                for hop in (8, 16, 32, 64):
                    value = value + pltpu.roll(value, hop, 1)
                spread.append(value)
            made = factors(*spread)
            for m in range(6):
                side_metric[side, m, rows, :] = made[m]
            wet = made[0] > (levels - 1 - group).astype(jnp.float32)
            for f in range(4):
                sides[side, f, rows, :] = jnp.where(wet, strips[side, f, rows, :], 0.0)

    @pl.loop(0, height // 8)
    def _(tile):
        side_tables(pl.ds(pl.multiple_of(tile * 8, 8), 8))

    go_east.wait_send()
    go_west.wait_send()
    rows_in(*main)

    def mirrored(value, index):
        pieces = [
            jnp.take_along_axis(value[i : i + 8, :], index, axis=1)
            for i in range(0, value.shape[0], 8)
        ]
        return jnp.concatenate(pieces, axis=0)

    signs = (1.0, 1.0, -1.0, -1.0)
    safe = (0.0, 1.0, 1.0, 0.0)
    turn = width - 1 - lane
    far, near = rows_n[base : base + 16, :], rows_s[base : base + 16, :]
    flipped = mirrored(far, turn)
    for k in range(RIM):
        up = [
            jnp.where(
                last,
                flipped[m * RIM + RIM - 1 - k : m * RIM + RIM - k, :],
                far[m * RIM + k : m * RIM + k + 1, :],
            )
            for m in range(4)
        ]
        down = [
            jnp.where(bottom, safe[m], near[m * RIM + k : m * RIM + k + 1, :]) for m in range(4)
        ]
        for at, raw in ((RIM + height + k, up), (k, down)):
            made = factors(*raw)
            for m in range(6):
                table[m, at, :, :] = jnp.broadcast_to(made[m], (8, width))
        for half in range(levels // 8):
            wet_up, wet_down = wet_of(RIM + height + k, half), wet_of(k, half)
            for f in range(4):
                span = slice(8 * half, 8 * half + 8)
                at = (f * RIM + k) * levels + 8 * half
                fold = (f * RIM + RIM - 1 - k) * levels + 8 * half
                turned = signs[f] * jnp.take_along_axis(rows_n[fold : fold + 8, :], turn, axis=1)
                value = jnp.where(last, turned, rows_n[at : at + 8, :])
                state[f, RIM + height + k, span, :] = jnp.where(wet_up, value, 0.0)
                state[f, k, span, :] = jnp.where(wet_down, rows_s[at : at + 8, :], 0.0)

    rows_in(*ends)
    side_far = strip_n[...]
    side_flipped = mirrored(side_far, group * 8 + jnp.where(within < 6, 5 - within, within))
    side_near = strip_s[...]
    for side in range(2):
        for f in range(5):
            if f == 4:
                fill = jnp.where((group == 1) | (group == 2), 1.0, 0.0)
            else:
                fill = jnp.zeros((8, width), jnp.float32)
            strips[side, f, height:deep, :] = fill
            for r in range(RIM):
                at = (side * 5 + f) * RIM + r
                fold = ((1 - side) * 5 + f) * RIM + RIM - 1 - r
                sign = 1.0 if f == 4 else signs[f]
                strips[side, f, height + r : height + r + 1, :] = jnp.where(
                    last, sign * side_flipped[fold : fold + 1, :], side_far[at : at + 1, :]
                )
                got = side_near[at : at + 1, :]
                if f == 4:
                    got = jnp.where(bottom, fill[0:1, :], got)
                strips[side, f, deep - RIM + r : deep - RIM + r + 1, :] = got
    side_tables(slice(height, deep))
    rows_sent(*main)
    rows_sent(*ends)


def substeps(
    state, table, sides, side_metric, mixing,
    y0, y1, y2, y3,
    second, third, result, sides_second, sides_third, link, store_sem,
):
    outs = (y0, y1, y2, y3)
    rows_deep, levels, width = state.shape[1:]
    height = rows_deep - 2 * RIM
    halves = levels // 8
    tiles = sides.shape[2] // 8
    lane = lanes((8, width))
    row = lax.broadcasted_iota(jnp.int32, (8, width), 0)
    group = lane // 8
    within = lane - group * 8

    mixes = [(mixing[h], mixing[halves + 1 + h]) for h in range(halves)]
    numbers = [(row + 8 * h).astype(jnp.float32) for h in range(halves)]

    def update(centre, easts, wests, norths, souths, factor, number, mix):
        bath, a2, b2, ah, bh, vo = factor
        wet = bath > number
        a2 = jnp.where(wet, a2, 0.0)
        b2 = jnp.where(wet, b2, 0.0)
        u, v = centre[2], centre[3]
        du, dv = u * ah, v * bh
        results = []
        for f in range(4):
            if f % 2 == 0:
                da, db = mix[f // 2] * a2, mix[f // 2] * b2
                ce, cw, cn, cs = da - du, da + du, db - dv, db + dv
                cc = 1.0 - 2.0 * (da + db)
            new = cc * centre[f] + (ce * easts[f] + cw * wests[f])
            new = new + (cn * norths[f] + cs * souths[f])
            if f == 2:
                new = new + vo * v
            if f == 3:
                new = new - vo * u
            results.append(new)
        return results

    def main_step(source, store, low, high, unroll):
        @pl.loop(low, high, unroll=unroll)
        def _(r):
            factor = [table[m, r, :, :] for m in range(6)]
            seam_row = lax.rem(r + 8 * tiles - RIM, 8 * tiles)
            seams = [
                jnp.broadcast_to(link[f, pl.ds(seam_row, 1), :], (8, width)) for f in range(4)
            ]
            for half in range(halves):
                span = slice(8 * half, 8 * half + 8)
                centre = [source[f, r, span, :] for f in range(4)]
                easts, wests = [], []
                for f in range(4):
                    z = pltpu.roll(seams[f], width - 3 - 8 * (levels - 1) + 64 * half, 1, stride=8, stride_axis=0)
                    easts.append(pltpu.roll(jnp.where(lane == 0, z, centre[f]), width - 1, 1))
                    wests.append(pltpu.roll(jnp.where(lane == width - 1, z, centre[f]), 1, 1))
                norths = [source[f, r + 1, span, :] for f in range(4)]
                souths = [source[f, r - 1, span, :] for f in range(4)]
                new = update(centre, easts, wests, norths, souths, factor, numbers[half], mixes[half])
                for f in range(4):
                    store(f, r, half, new[f])

    def side_step(source, target):
        mix = (mixing[halves], mixing[2 * halves + 1])
        number = (levels - 1 - group).astype(jnp.float32)
        for side in range(2):
            for t in range(tiles):
                rows = slice(8 * t, 8 * t + 8)
                prior, following = (t + tiles - 1) % tiles * 8, (t + 1) % tiles * 8
                centre = [source[side, f, rows, :] for f in range(4)]
                easts = [pltpu.roll(c, width - 1, 1) for c in centre]
                wests = [pltpu.roll(c, 1, 1) for c in centre]
                norths = [
                    jnp.where(
                        row == 7,
                        pltpu.roll(source[side, f, following : following + 8, :], 7, 0),
                        pltpu.roll(centre[f], 7, 0),
                    )
                    for f in range(4)
                ]
                souths = [
                    jnp.where(
                        row == 0,
                        pltpu.roll(source[side, f, prior : prior + 8, :], 1, 0),
                        pltpu.roll(centre[f], 1, 0),
                    )
                    for f in range(4)
                ]
                factor = [side_metric[side, m, rows, :] for m in range(6)]
                new = update(centre, easts, wests, norths, souths, factor, number, mix)
                for f in range(4):
                    target[side, f, rows, :] = new[f]

    def join(source):
        for f in range(4):
            for t in range(tiles):
                rows = slice(8 * t, 8 * t + 8)
                link[f, rows, :] = jnp.where(within == 2, source[0, f, rows, :], source[1, f, rows, :])

    def into(buffer):
        def store(f, r, half, value):
            buffer[f, r, 8 * half : 8 * half + 8, :] = value
        return store

    def final(f, r, half, value):
        result[f, pl.ds(r - RIM + half * 8 * height, 8, stride=height), :] = value

    def split(count):
        return max(n for n in range(1, 18) if count % n == 0)

    join(sides)
    main_step(state, into(second), 1, rows_deep - 1, split(rows_deep - 2))
    side_step(sides, sides_second)
    join(sides_second)
    main_step(second, into(third), 2, rows_deep - 2, split(rows_deep - 4))
    side_step(sides_second, sides_third)
    join(sides_third)
    main_step(third, final, 3, rows_deep - 3, split(rows_deep - 6))
    stores = [
        pltpu.make_async_copy(result.at[f], outs[f], store_sem.at[f]) for f in range(4)
    ]
    for copy in stores:
        copy.start()
    for copy in stores:
        copy.wait()


def on_device(
    potential_heat_state,
    saltiness_anomaly,
    first_current_component,
    second_current_component,
    bathymetry_layer_total,
    westeast_cell_extent,
    southnorth_cell_extent,
    planetary_vorticity,
    scalar_mixing_factor,
    momentum_mixing_factor,
):
    fields = (potential_heat_state, saltiness_anomaly, first_current_component, second_current_component)
    metrics = (bathymetry_layer_total, westeast_cell_extent, southnorth_cell_extent, planetary_vorticity)
    levels, height, width = potential_heat_state.shape
    f32 = jnp.float32
    message = 4 * RIM * levels + 16
    deep = height + 8
    flat = (levels * height, width)
    vmem = pl.BlockSpec(memory_space=pltpu.VMEM)
    anywhere = pl.BlockSpec(memory_space=pltpu.HBM)
    laid = pl.pallas_call(
        exchange,
        out_shape=(
            pltpu.VMEM((4, height + 2 * RIM, levels, width), f32),
            pltpu.VMEM((6, height + 2 * RIM, 8, width), f32),
            pltpu.VMEM((2, 4, deep, width), f32),
            pltpu.VMEM((2, 6, deep, width), f32),
            pltpu.VMEM((2 * (levels // 8 + 1), 8, width), f32),
        ),
        in_specs=[anywhere] * 10,
        out_specs=[vmem] * 5,
        scratch_shapes=[
            pltpu.SMEM((levels,), f32),
            pltpu.SMEM((levels,), f32),
            pltpu.VMEM((4,) + flat, f32),
            pltpu.VMEM((3, height, width), f32),
            pltpu.VMEM((height, width), jnp.int32),
            pltpu.VMEM((4, height, width), f32),
            pltpu.VMEM((message, width), f32),
            pltpu.VMEM((message, width), f32),
            pltpu.VMEM((2, 5, deep, width), f32),
            pltpu.VMEM((32, width), f32),
            pltpu.VMEM((32, width), f32),
            pltpu.VMEM((message, width), f32),
            pltpu.VMEM((message, width), f32),
            pltpu.VMEM((5, height, width), f32),
            pltpu.VMEM((2, 3, height, width), f32),
            pltpu.VMEM((2, 3, height, width), f32),
            pltpu.VMEM((32, width), f32),
            pltpu.VMEM((32, width), f32),
            pltpu.SemaphoreType.DMA((6,)),
            pltpu.SemaphoreType.DMA((6,)),
            pltpu.SemaphoreType.DMA((10,)),
        ],
        compiler_params=pltpu.CompilerParams(
            collective_id=0, has_side_effects=True, vmem_limit_bytes=int(59.36 * 2**20)
        ),
        name="exchange",
    )(*[x.reshape(flat) for x in fields], *metrics, scalar_mixing_factor, momentum_mixing_factor)
    news = pl.pallas_call(
        substeps,
        out_shape=(jax.ShapeDtypeStruct(flat, f32),) * 4,
        in_specs=[vmem] * 5,
        out_specs=[anywhere] * 4,
        scratch_shapes=[
            pltpu.VMEM((4, height + 2 * RIM, levels, width), f32),
            pltpu.VMEM((4, height + 2 * RIM, levels, width), f32),
            pltpu.VMEM((4,) + flat, f32),
            pltpu.VMEM((2, 4, deep, width), f32),
            pltpu.VMEM((2, 4, deep, width), f32),
            pltpu.VMEM((4, deep, width), f32),
            pltpu.SemaphoreType.DMA((4,)),
        ],
        compiler_params=pltpu.CompilerParams(vmem_limit_bytes=24 * 2**20),
        name="substeps",
    )(*laid)
    return tuple(x.reshape((levels, height, width)) for x in news)


def solution(mesh):
    state, plane = P(None, "lat", "lon"), P("lat", "lon")
    return jax.shard_map(
        on_device,
        mesh=mesh,
        in_specs=(state,) * 4 + (plane,) * 4 + (P(), P()),
        out_specs=(state,) * 4,
        check_vma=False,
    )
```

```python
import functools

import jax
import jax.numpy as jnp
from jax import lax
from jax.experimental import pallas as pl
from jax.experimental.pallas import tpu as pltpu
from jax.sharding import PartitionSpec as P

STEPS = 3
RIM = 3
time_step = 0.2

MESH = pl.DeviceIdType.MESH


def lanes(shape):
    return lax.broadcasted_iota(jnp.int32, shape, len(shape) - 1)


def factors(bath, we, sn, vo):
    a, b = 1.0 / we, 1.0 / sn
    return (
        bath, time_step * a * a, time_step * b * b,
        0.5 * time_step * a, 0.5 * time_step * b, time_step * vo,
    )


def exchange(
    x0, x1, x2, x3, bathy, wide, high, vort, tracer_mix, momentum_mix,
    state, table, sides, side_metric, mixing,
    factor_t, factor_m, field, whole, bath, metric,
    rows_n, rows_s, strips, strip_n, strip_s,
    out_n, out_s, packed, to_side, from_side, edge_n, edge_s,
    send_sem, recv_sem, load_sem,
):
    levels, width = state.shape[2], state.shape[3]
    height = wide.shape[0]
    deep = height + 8
    lat, lon = lax.axis_index("lat"), lax.axis_index("lon")
    lats, lons = lax.axis_size("lat"), lax.axis_size("lon")
    last, bottom = lat == lats - 1, lat == 0
    east = (lat, lax.rem(lon + 1, lons))
    west = (lat, lax.rem(lon + lons - 1, lons))
    north = (
        jnp.where(last, lat, lat + 1),
        jnp.where(last, lons - 1 - lon, lon),
    )
    south = (lat - 1, lon)

    loads = [
        pltpu.make_async_copy(x, field.at[f], load_sem.at[f]) for f, x in enumerate((x0, x1, x2, x3))
    ]
    loads.append(pltpu.make_async_copy(bathy, bath, load_sem.at[4]))
    loads += [
        pltpu.make_async_copy(x, whole.at[m], load_sem.at[5 + m]) for m, x in enumerate((wide, high, vort))
    ]
    loads += [
        pltpu.make_async_copy(tracer_mix, factor_t, load_sem.at[8]),
        pltpu.make_async_copy(momentum_mix, factor_m, load_sem.at[9]),
    ]
    for load in loads:
        load.start()

    barrier = pltpu.get_barrier_semaphore()
    for peer in (east, west, north):
        pl.semaphore_signal(barrier, inc=1, device_id=peer, device_id_type=MESH)

    @pl.when(lat > 0)
    def _():
        pl.semaphore_signal(barrier, inc=1, device_id=south, device_id_type=MESH)

    lane = lanes((8, width))
    row = lax.broadcasted_iota(jnp.int32, (8, width), 0)
    group = lane // 8
    within = lane - group * 8
    for load in loads:
        load.wait()

    @pl.loop(0, height // 8)
    def _(tile):
        start = pl.multiple_of(tile * 8, 8)
        rows = pl.ds(start, 8)
        cols = []
        for f in range(4):
            acc = pltpu.roll(field[f, rows, :], 8 * (levels - 1) + RIM, 1)
            for level in range(1, levels):
                spot = levels - 1 - level
                at = pl.ds(pl.multiple_of(start + level * height, 8), 8)
                acc = jnp.where(group == spot, pltpu.roll(field[f, at, :], 8 * spot + RIM, 1), acc)
            packed[f, rows, :] = acc
            cols.append(acc)
        acc = jnp.zeros((8, width), jnp.float32)
        raw = (bath[rows, :].astype(jnp.float32), whole[0, rows, :], whole[1, rows, :], whole[2, rows, :])
        for m in range(4):
            metric[m, rows, :] = raw[m]
            acc = jnp.where(group == m, pltpu.roll(raw[m], 8 * m + RIM, 1), acc)
        packed[4, rows, :] = acc
        for pair in range(2):
            one, two = cols[2 * pair], cols[2 * pair + 1]
            to_side[0, pair, rows, :] = jnp.where(within < 4, one, pltpu.roll(two, 4, 1))
            to_side[1, pair, rows, :] = jnp.where(within < 3, pltpu.roll(two, width - 3, 1), one)
        to_side[0, 2, rows, :] = acc
        to_side[1, 2, rows, :] = acc

    @pl.when(lat > 0)
    def _():
        pl.semaphore_wait(barrier, 4)

    @pl.when(lat == 0)
    def _():
        pl.semaphore_wait(barrier, 3)

    def remote(src, dst, which, arrive, peer):
        return pltpu.make_async_remote_copy(
            src_ref=src, dst_ref=dst, send_sem=send_sem.at[which], recv_sem=recv_sem.at[arrive],
            device_id=peer, device_id_type=MESH,
        )

    go_east = remote(to_side.at[0], from_side.at[0], 0, 0, east)
    go_west = remote(to_side.at[1], from_side.at[1], 1, 1, west)
    go_east.start()
    go_west.start()

    def column(f, r, half):
        return field[f, pl.ds(r + half * 8 * height, 8, stride=height), :]

    for f in range(4):
        for r in range(RIM):
            at = (f * RIM + r) * levels
            for half in range(levels // 8):
                rows = slice(at + 8 * half, at + 8 * half + 8)
                out_s[rows, :] = column(f, r, half)
                out_n[rows, :] = column(f, height - RIM + r, half)
    base = 4 * RIM * levels
    out_s[base : base + 16, :] = jnp.zeros((16, width), jnp.float32)
    out_n[base : base + 16, :] = jnp.zeros((16, width), jnp.float32)
    for m in range(4):
        out_s[base + m * RIM : base + (m + 1) * RIM, :] = metric[m, 0:RIM, :]
        out_n[base + m * RIM : base + (m + 1) * RIM, :] = metric[m, height - RIM : height, :]

    def rows_out(to_n, to_s, recv_n, recv_s, first):
        up = remote(to_n, recv_s, first, first, north)
        fold = remote(to_n, recv_n, first, first + 1, north)
        down = remote(to_s, recv_n, first + 1, first + 1, south)

        @pl.when(last)
        def _():
            fold.start()

        @pl.when(lat < lats - 1)
        def _():
            up.start()

        @pl.when(lat > 0)
        def _():
            down.start()

        return up, down

    def rows_in(up, down):
        down.wait_recv()

        @pl.when(lat > 0)
        def _():
            up.wait_recv()

    def rows_sent(up, down):
        up.wait_send()

        @pl.when(lat > 0)
        def _():
            down.wait_send()

    @pl.when(lat == 0)
    def _():
        rows_s[...] = jnp.zeros(rows_s.shape, jnp.float32)
        strip_s[...] = jnp.zeros(strip_s.shape, jnp.float32)

    main = rows_out(out_n, out_s, rows_n, rows_s, 2)

    @pl.loop(0, height // 8)
    def _(tile):
        rows = pl.ds(pl.multiple_of(tile * 8, 8), 8)
        made = factors(*[metric[m, rows, :] for m in range(4)])
        for m in range(6):
            for i in range(8):
                table[m, RIM + tile * 8 + i, :, :] = jnp.broadcast_to(made[m][i : i + 1, :], (8, width))

    def wet_of(at, half):
        return table[0, at, :, :] > (row + 8 * half).astype(jnp.float32)

    go_east.wait_recv()
    go_west.wait_recv()

    @pl.loop(0, height // 8)
    def _(tile):
        rows = pl.ds(pl.multiple_of(tile * 8, 8), 8)
        for f in range(5):
            own = packed[f, rows, :]
            got_w = from_side[0, f // 2, rows, :]
            got_e = from_side[1, f // 2, rows, :]
            if f % 2 == 1:
                got_w = pltpu.roll(got_w, width - 4, 1)
                got_e = pltpu.roll(got_e, 3, 1)
            strips[0, f, rows, :] = jnp.where(within < RIM, got_w, own)
            strips[1, f, rows, :] = jnp.where(within < RIM, own, got_e)

    edge_n[30:32, :] = jnp.zeros((2, width), jnp.float32)
    edge_s[30:32, :] = jnp.zeros((2, width), jnp.float32)
    for side in range(2):
        for f in range(5):
            at = (side * 5 + f) * RIM
            edge_s[at : at + RIM, :] = strips[side, f, 0:RIM, :]
            edge_n[at : at + RIM, :] = strips[side, f, height - RIM : height, :]
    ends = rows_out(edge_n, edge_s, strip_n, strip_s, 4)

    @pl.loop(0, height, unroll=8)
    def _(r):
        for half in range(levels // 8):
            wet = wet_of(RIM + r, half)
            for f in range(4):
                state[f, RIM + r, 8 * half : 8 * half + 8, :] = jnp.where(wet, column(f, r, half), 0.0)

    for k, mix in enumerate((factor_t, factor_m)):
        spread = jnp.zeros((8, width), jnp.float32)
        for half in range(levels // 8):
            value = jnp.zeros((8, width), jnp.float32)
            for i in range(8):
                value = jnp.where(row == i, mix[8 * half + i], value)
                spread = jnp.where(group == levels - 1 - 8 * half - i, mix[8 * half + i], spread)
            mixing[(levels // 8 + 1) * k + half] = value
        mixing[(levels // 8 + 1) * k + levels // 8] = spread

    def side_tables(rows):
        for side in range(2):
            mixed = strips[side, 4, rows, :]
            spread = []
            for m in range(4):
                value = jnp.where(group == m, mixed, 0.0)
                for hop in (8, 16, 32, 64):
                    value = value + pltpu.roll(value, hop, 1)
                spread.append(value)
            made = factors(*spread)
            for m in range(6):
                side_metric[side, m, rows, :] = made[m]
            wet = made[0] > (levels - 1 - group).astype(jnp.float32)
            for f in range(4):
                sides[side, f, rows, :] = jnp.where(wet, strips[side, f, rows, :], 0.0)

    @pl.loop(0, height // 8)
    def _(tile):
        side_tables(pl.ds(pl.multiple_of(tile * 8, 8), 8))

    go_east.wait_send()
    go_west.wait_send()
    rows_in(*main)

    def mirrored(value, index):
        pieces = [
            jnp.take_along_axis(value[i : i + 8, :], index, axis=1)
            for i in range(0, value.shape[0], 8)
        ]
        return jnp.concatenate(pieces, axis=0)

    signs = (1.0, 1.0, -1.0, -1.0)
    safe = (0.0, 1.0, 1.0, 0.0)
    turn = width - 1 - lane
    far, near = rows_n[base : base + 16, :], rows_s[base : base + 16, :]
    flipped = mirrored(far, turn)
    for k in range(RIM):
        up = [
            jnp.where(
                last,
                flipped[m * RIM + RIM - 1 - k : m * RIM + RIM - k, :],
                far[m * RIM + k : m * RIM + k + 1, :],
            )
            for m in range(4)
        ]
        down = [
            jnp.where(bottom, safe[m], near[m * RIM + k : m * RIM + k + 1, :]) for m in range(4)
        ]
        for at, raw in ((RIM + height + k, up), (k, down)):
            made = factors(*raw)
            for m in range(6):
                table[m, at, :, :] = jnp.broadcast_to(made[m], (8, width))
        for half in range(levels // 8):
            wet_up, wet_down = wet_of(RIM + height + k, half), wet_of(k, half)
            for f in range(4):
                span = slice(8 * half, 8 * half + 8)
                at = (f * RIM + k) * levels + 8 * half
                fold = (f * RIM + RIM - 1 - k) * levels + 8 * half
                turned = signs[f] * jnp.take_along_axis(rows_n[fold : fold + 8, :], turn, axis=1)
                value = jnp.where(last, turned, rows_n[at : at + 8, :])
                state[f, RIM + height + k, span, :] = jnp.where(wet_up, value, 0.0)
                state[f, k, span, :] = jnp.where(wet_down, rows_s[at : at + 8, :], 0.0)

    rows_in(*ends)
    side_far = strip_n[...]
    side_flipped = mirrored(side_far, group * 8 + jnp.where(within < 6, 5 - within, within))
    side_near = strip_s[...]
    for side in range(2):
        for f in range(5):
            if f == 4:
                fill = jnp.where((group == 1) | (group == 2), 1.0, 0.0)
            else:
                fill = jnp.zeros((8, width), jnp.float32)
            strips[side, f, height:deep, :] = fill
            for r in range(RIM):
                at = (side * 5 + f) * RIM + r
                fold = ((1 - side) * 5 + f) * RIM + RIM - 1 - r
                sign = 1.0 if f == 4 else signs[f]
                strips[side, f, height + r : height + r + 1, :] = jnp.where(
                    last, sign * side_flipped[fold : fold + 1, :], side_far[at : at + 1, :]
                )
                got = side_near[at : at + 1, :]
                if f == 4:
                    got = jnp.where(bottom, fill[0:1, :], got)
                strips[side, f, deep - RIM + r : deep - RIM + r + 1, :] = got
    side_tables(slice(height, deep))
    rows_sent(*main)
    rows_sent(*ends)


def substeps(
    state, table, sides, side_metric, mixing,
    y0, y1, y2, y3,
    second, third, result, sides_second, sides_third, seam, easts, wests, store_sem,
):
    outs = (y0, y1, y2, y3)
    rows_deep, levels, width = state.shape[1:]
    height = rows_deep - 2 * RIM
    halves = levels // 8
    tiles = sides.shape[2] // 8
    lane = lanes((8, width))
    row = lax.broadcasted_iota(jnp.int32, (8, width), 0)
    group = lane // 8
    within = lane - group * 8

    mixes = [(mixing[h], mixing[halves + 1 + h]) for h in range(halves)]
    numbers = [(row + 8 * h).astype(jnp.float32) for h in range(halves)]

    def update(centre, easts, wests, norths, souths, factor, number, mix):
        bath, a2, b2, ah, bh, vo = factor
        wet = bath > number
        a2 = jnp.where(wet, a2, 0.0)
        b2 = jnp.where(wet, b2, 0.0)
        u, v = centre[2], centre[3]
        du, dv = u * ah, v * bh
        results = []
        for f in range(4):
            if f % 2 == 0:
                da, db = mix[f // 2] * a2, mix[f // 2] * b2
                ce, cw, cn, cs = da - du, da + du, db - dv, db + dv
                cc = 1.0 - 2.0 * (da + db)
            new = cc * centre[f] + (ce * easts[f] + cw * wests[f])
            new = new + (cn * norths[f] + cs * souths[f])
            if f == 2:
                new = new + vo * v
            if f == 3:
                new = new - vo * u
            results.append(new)
        return results

    def main_step(source, store, low, high):
        @pl.loop(low, high, unroll=2)
        def _(r):
            seam_row = lax.rem(r + 8 * tiles - RIM, 8 * tiles) * levels
            for half in range(halves):
                span = slice(8 * half, 8 * half + 8)
                place = pl.ds(pl.multiple_of(seam_row + 8 * half, 8), 8)
                for f in range(4):
                    z, c = seam[f, place, :], source[f, r, span, :]
                    easts[f, r, span, :] = pltpu.roll(jnp.where(lane == 0, z, c), width - 1, 1)
                    wests[f, r, span, :] = pltpu.roll(jnp.where(lane == width - 1, z, c), 1, 1)

        @pl.loop(low, high)
        def _(r):
            factor = [table[m, r, :, :] for m in range(6)]
            for half in range(halves):
                span = slice(8 * half, 8 * half + 8)
                new = update(
                    [source[f, r, span, :] for f in range(4)],
                    [easts[f, r, span, :] for f in range(4)],
                    [wests[f, r, span, :] for f in range(4)],
                    [source[f, r + 1, span, :] for f in range(4)],
                    [source[f, r - 1, span, :] for f in range(4)],
                    factor, numbers[half], mixes[half],
                )
                for f in range(4):
                    store(f, r, half, new[f])

    def side_step(source, target):
        mix = (mixing[halves], mixing[2 * halves + 1])
        number = (levels - 1 - group).astype(jnp.float32)
        for side in range(2):
            for t in range(tiles):
                rows = slice(8 * t, 8 * t + 8)
                prior, following = (t + tiles - 1) % tiles * 8, (t + 1) % tiles * 8
                centre = [source[side, f, rows, :] for f in range(4)]
                easts = [pltpu.roll(c, width - 1, 1) for c in centre]
                wests = [pltpu.roll(c, 1, 1) for c in centre]
                norths = [
                    jnp.where(
                        row == 7,
                        pltpu.roll(source[side, f, following : following + 8, :], 7, 0),
                        pltpu.roll(centre[f], 7, 0),
                    )
                    for f in range(4)
                ]
                souths = [
                    jnp.where(
                        row == 0,
                        pltpu.roll(source[side, f, prior : prior + 8, :], 1, 0),
                        pltpu.roll(centre[f], 1, 0),
                    )
                    for f in range(4)
                ]
                factor = [side_metric[side, m, rows, :] for m in range(6)]
                new = update(centre, easts, wests, norths, souths, factor, number, mix)
                for f in range(4):
                    target[side, f, rows, :] = new[f]

    def join(source):
        @pl.loop(0, tiles)
        def _(t):
            rows = pl.ds(pl.multiple_of(t * 8, 8), 8)
            for f in range(4):
                z = jnp.where(within == 2, source[0, f, rows, :], source[1, f, rows, :])
                for level in range(levels):
                    spot = 8 * (levels - 1 - level) + 2
                    moved = pltpu.roll(z, width - 1 - spot, 1)
                    seam[f, pl.ds(t * 8 * levels + level, 8, stride=levels), :] = moved

    def into(buffer):
        def store(f, r, half, value):
            buffer[f, r, 8 * half : 8 * half + 8, :] = value
        return store

    def final(f, r, half, value):
        result[f, pl.ds(r - RIM + half * 8 * height, 8, stride=height), :] = value

    join(sides)
    main_step(state, into(second), 1, rows_deep - 1)
    side_step(sides, sides_second)
    join(sides_second)
    main_step(second, into(third), 2, rows_deep - 2)
    side_step(sides_second, sides_third)
    join(sides_third)
    main_step(third, final, 3, rows_deep - 3)
    stores = [
        pltpu.make_async_copy(result.at[f], outs[f], store_sem.at[f]) for f in range(4)
    ]
    for copy in stores:
        copy.start()
    for copy in stores:
        copy.wait()


def on_device(
    potential_heat_state,
    saltiness_anomaly,
    first_current_component,
    second_current_component,
    bathymetry_layer_total,
    westeast_cell_extent,
    southnorth_cell_extent,
    planetary_vorticity,
    scalar_mixing_factor,
    momentum_mixing_factor,
):
    fields = (potential_heat_state, saltiness_anomaly, first_current_component, second_current_component)
    metrics = (bathymetry_layer_total, westeast_cell_extent, southnorth_cell_extent, planetary_vorticity)
    levels, height, width = potential_heat_state.shape
    f32 = jnp.float32
    message = 4 * RIM * levels + 16
    deep = height + 8
    flat = (levels * height, width)
    vmem = pl.BlockSpec(memory_space=pltpu.VMEM)
    anywhere = pl.BlockSpec(memory_space=pltpu.HBM)
    laid = pl.pallas_call(
        exchange,
        out_shape=(
            pltpu.VMEM((4, height + 2 * RIM, levels, width), f32),
            pltpu.VMEM((6, height + 2 * RIM, 8, width), f32),
            pltpu.VMEM((2, 4, deep, width), f32),
            pltpu.VMEM((2, 6, deep, width), f32),
            pltpu.VMEM((2 * (levels // 8 + 1), 8, width), f32),
        ),
        in_specs=[anywhere] * 10,
        out_specs=[vmem] * 5,
        scratch_shapes=[
            pltpu.SMEM((levels,), f32),
            pltpu.SMEM((levels,), f32),
            pltpu.VMEM((4,) + flat, f32),
            pltpu.VMEM((3, height, width), f32),
            pltpu.VMEM((height, width), jnp.int32),
            pltpu.VMEM((4, height, width), f32),
            pltpu.VMEM((message, width), f32),
            pltpu.VMEM((message, width), f32),
            pltpu.VMEM((2, 5, deep, width), f32),
            pltpu.VMEM((32, width), f32),
            pltpu.VMEM((32, width), f32),
            pltpu.VMEM((message, width), f32),
            pltpu.VMEM((message, width), f32),
            pltpu.VMEM((5, height, width), f32),
            pltpu.VMEM((2, 3, height, width), f32),
            pltpu.VMEM((2, 3, height, width), f32),
            pltpu.VMEM((32, width), f32),
            pltpu.VMEM((32, width), f32),
            pltpu.SemaphoreType.DMA((6,)),
            pltpu.SemaphoreType.DMA((6,)),
            pltpu.SemaphoreType.DMA((10,)),
        ],
        compiler_params=pltpu.CompilerParams(
            collective_id=0, has_side_effects=True, vmem_limit_bytes=int(59.36 * 2**20)
        ),
        name="exchange",
    )(*[x.reshape(flat) for x in fields], *metrics, scalar_mixing_factor, momentum_mixing_factor)
    news = pl.pallas_call(
        substeps,
        out_shape=(jax.ShapeDtypeStruct(flat, f32),) * 4,
        in_specs=[vmem] * 5,
        out_specs=[anywhere] * 4,
        scratch_shapes=[
            pltpu.VMEM((4, height + 2 * RIM, levels, width), f32),
            pltpu.VMEM((4, height + 2 * RIM, levels, width), f32),
            pltpu.VMEM((4,) + flat, f32),
            pltpu.VMEM((2, 4, deep, width), f32),
            pltpu.VMEM((2, 4, deep, width), f32),
            pltpu.VMEM((4, deep * levels, width), f32),
            pltpu.VMEM((4, height + 2 * RIM, levels, width), f32),
            pltpu.VMEM((4, height + 2 * RIM, levels, width), f32),
            pltpu.SemaphoreType.DMA((4,)),
        ],
        compiler_params=pltpu.CompilerParams(vmem_limit_bytes=32 * 2**20),
        name="substeps",
    )(*laid)
    return tuple(x.reshape((levels, height, width)) for x in news)


def solution(mesh):
    state, plane = P(None, "lat", "lon"), P("lat", "lon")
    return jax.shard_map(
        on_device,
        mesh=mesh,
        in_specs=(state,) * 4 + (plane,) * 4 + (P(), P()),
        out_specs=(state,) * 4,
        check_vma=False,
    )
```

```python
import functools

import jax
import jax.numpy as jnp
from jax import lax
from jax.experimental import pallas as pl
from jax.experimental.pallas import tpu as pltpu
from jax.sharding import PartitionSpec as P

STEPS = 3
RIM = 3
time_step = 0.2

MESH = pl.DeviceIdType.MESH


def lanes(shape):
    return lax.broadcasted_iota(jnp.int32, shape, len(shape) - 1)


def factors(bath, we, sn, vo):
    a, b = 1.0 / we, 1.0 / sn
    return (
        bath, time_step * a * a, time_step * b * b,
        0.5 * time_step * a, 0.5 * time_step * b, time_step * vo,
    )


def exchange(
    x0, x1, x2, x3, bathy, wide, high, vort, tracer_mix, momentum_mix,
    state, table, sides, side_metric, mixing,
    factor_t, factor_m, field, whole, bath, metric,
    rows_n, rows_s, strips, strip_n, strip_s,
    out_n, out_s, packed, to_side, from_side, edge_n, edge_s,
    send_sem, recv_sem, load_sem,
):
    levels, width = state.shape[1], state.shape[3]
    height = wide.shape[0]
    deep = height + 8
    lat, lon = lax.axis_index("lat"), lax.axis_index("lon")
    lats, lons = lax.axis_size("lat"), lax.axis_size("lon")
    last, bottom = lat == lats - 1, lat == 0
    east = (lat, lax.rem(lon + 1, lons))
    west = (lat, lax.rem(lon + lons - 1, lons))
    north = (
        jnp.where(last, lat, lat + 1),
        jnp.where(last, lons - 1 - lon, lon),
    )
    south = (lat - 1, lon)

    loads = [
        pltpu.make_async_copy(x, field.at[f], load_sem.at[f]) for f, x in enumerate((x0, x1, x2, x3))
    ]
    loads.append(pltpu.make_async_copy(bathy, bath, load_sem.at[4]))
    loads += [
        pltpu.make_async_copy(x, whole.at[m], load_sem.at[5 + m]) for m, x in enumerate((wide, high, vort))
    ]
    loads += [
        pltpu.make_async_copy(tracer_mix, factor_t, load_sem.at[8]),
        pltpu.make_async_copy(momentum_mix, factor_m, load_sem.at[9]),
    ]
    for load in loads:
        load.start()

    barrier = pltpu.get_barrier_semaphore()
    for peer in (east, west, north):
        pl.semaphore_signal(barrier, inc=1, device_id=peer, device_id_type=MESH)

    @pl.when(lat > 0)
    def _():
        pl.semaphore_signal(barrier, inc=1, device_id=south, device_id_type=MESH)

    lane = lanes((8, width))
    row = lax.broadcasted_iota(jnp.int32, (8, width), 0)
    group = lane // 8
    within = lane - group * 8
    for load in loads:
        load.wait()

    @pl.loop(0, height // 8)
    def _(tile):
        start = pl.multiple_of(tile * 8, 8)
        rows = pl.ds(start, 8)
        cols = []
        for f in range(4):
            acc = pltpu.roll(field[f, rows, :], 8 * (levels - 1) + RIM, 1)
            for level in range(1, levels):
                spot = levels - 1 - level
                at = pl.ds(pl.multiple_of(start + level * height, 8), 8)
                acc = jnp.where(group == spot, pltpu.roll(field[f, at, :], 8 * spot + RIM, 1), acc)
            packed[f, rows, :] = acc
            cols.append(acc)
        acc = jnp.zeros((8, width), jnp.float32)
        raw = (bath[rows, :].astype(jnp.float32), whole[0, rows, :], whole[1, rows, :], whole[2, rows, :])
        for m in range(4):
            metric[m, rows, :] = raw[m]
            acc = jnp.where(group == m, pltpu.roll(raw[m], 8 * m + RIM, 1), acc)
        packed[4, rows, :] = acc
        for pair in range(2):
            one, two = cols[2 * pair], cols[2 * pair + 1]
            to_side[0, pair, rows, :] = jnp.where(within < 4, one, pltpu.roll(two, 4, 1))
            to_side[1, pair, rows, :] = jnp.where(within < 3, pltpu.roll(two, width - 3, 1), one)
        to_side[0, 2, rows, :] = acc
        to_side[1, 2, rows, :] = acc

    @pl.when(lat > 0)
    def _():
        pl.semaphore_wait(barrier, 4)

    @pl.when(lat == 0)
    def _():
        pl.semaphore_wait(barrier, 3)

    def remote(src, dst, which, arrive, peer):
        return pltpu.make_async_remote_copy(
            src_ref=src, dst_ref=dst, send_sem=send_sem.at[which], recv_sem=recv_sem.at[arrive],
            device_id=peer, device_id_type=MESH,
        )

    go_east = remote(to_side.at[0], from_side.at[0], 0, 0, east)
    go_west = remote(to_side.at[1], from_side.at[1], 1, 1, west)
    go_east.start()
    go_west.start()

    def column(f, r, half):
        return field[f, pl.ds(r + half * 8 * height, 8, stride=height), :]

    for f in range(4):
        for r in range(RIM):
            at = (f * RIM + r) * levels
            for half in range(levels // 8):
                rows = slice(at + 8 * half, at + 8 * half + 8)
                out_s[rows, :] = column(f, r, half)
                out_n[rows, :] = column(f, height - RIM + r, half)
    base = 4 * RIM * levels
    out_s[base : base + 16, :] = jnp.zeros((16, width), jnp.float32)
    out_n[base : base + 16, :] = jnp.zeros((16, width), jnp.float32)
    for m in range(4):
        out_s[base + m * RIM : base + (m + 1) * RIM, :] = metric[m, 0:RIM, :]
        out_n[base + m * RIM : base + (m + 1) * RIM, :] = metric[m, height - RIM : height, :]

    def rows_out(to_n, to_s, recv_n, recv_s, first):
        up = remote(to_n, recv_s, first, first, north)
        fold = remote(to_n, recv_n, first, first + 1, north)
        down = remote(to_s, recv_n, first + 1, first + 1, south)

        @pl.when(last)
        def _():
            fold.start()

        @pl.when(lat < lats - 1)
        def _():
            up.start()

        @pl.when(lat > 0)
        def _():
            down.start()

        return up, down

    def rows_in(up, down):
        down.wait_recv()

        @pl.when(lat > 0)
        def _():
            up.wait_recv()

    def rows_sent(up, down):
        up.wait_send()

        @pl.when(lat > 0)
        def _():
            down.wait_send()

    @pl.when(lat == 0)
    def _():
        rows_s[...] = jnp.zeros(rows_s.shape, jnp.float32)
        strip_s[...] = jnp.zeros(strip_s.shape, jnp.float32)

    main = rows_out(out_n, out_s, rows_n, rows_s, 2)

    @pl.loop(0, height // 8)
    def _(tile):
        rows = pl.ds(pl.multiple_of(tile * 8, 8), 8)
        made = factors(*[metric[m, rows, :] for m in range(4)])
        for m in range(6):
            table[m, rows, :] = made[m]

    go_east.wait_recv()
    go_west.wait_recv()

    @pl.loop(0, height // 8)
    def _(tile):
        rows = pl.ds(pl.multiple_of(tile * 8, 8), 8)
        for f in range(5):
            own = packed[f, rows, :]
            got_w = from_side[0, f // 2, rows, :]
            got_e = from_side[1, f // 2, rows, :]
            if f % 2 == 1:
                got_w = pltpu.roll(got_w, width - 4, 1)
                got_e = pltpu.roll(got_e, 3, 1)
            strips[0, f, rows, :] = jnp.where(within < RIM, got_w, own)
            strips[1, f, rows, :] = jnp.where(within < RIM, own, got_e)

    edge_n[30:32, :] = jnp.zeros((2, width), jnp.float32)
    edge_s[30:32, :] = jnp.zeros((2, width), jnp.float32)
    for side in range(2):
        for f in range(5):
            at = (side * 5 + f) * RIM
            edge_s[at : at + RIM, :] = strips[side, f, 0:RIM, :]
            edge_n[at : at + RIM, :] = strips[side, f, height - RIM : height, :]
    ends = rows_out(edge_n, edge_s, strip_n, strip_s, 4)

    @pl.loop(0, levels)
    def _(level):
        number = level.astype(jnp.float32)
        for t in range(height // 8):
            wet = table[0, 8 * t : 8 * t + 8, :] > number
            at = pl.ds(pl.multiple_of(level * height + 8 * t, 8), 8)
            for f in range(4):
                state[f, level, 8 * t : 8 * t + 8, :] = jnp.where(wet, field[f, at, :], 0.0)

    for k, mix in enumerate((factor_t, factor_m)):
        spread = jnp.zeros((8, width), jnp.float32)
        for level in range(levels):
            spread = jnp.where(group == levels - 1 - level, mix[level], spread)
            mixing[k, level] = jnp.full((8, width), mix[level], jnp.float32)
        mixing[k, levels] = spread

    def side_tables(rows):
        for side in range(2):
            mixed = strips[side, 4, rows, :]
            spread = []
            for m in range(4):
                value = jnp.where(group == m, mixed, 0.0)
                for hop in (8, 16, 32, 64):
                    value = value + pltpu.roll(value, hop, 1)
                spread.append(value)
            made = factors(*spread)
            for m in range(6):
                side_metric[side, m, rows, :] = made[m]
            wet = made[0] > (levels - 1 - group).astype(jnp.float32)
            for f in range(4):
                sides[side, f, rows, :] = jnp.where(wet, strips[side, f, rows, :], 0.0)

    @pl.loop(0, height // 8)
    def _(tile):
        side_tables(pl.ds(pl.multiple_of(tile * 8, 8), 8))

    go_east.wait_send()
    go_west.wait_send()
    rows_in(*main)

    def mirrored(value, index):
        pieces = [
            jnp.take_along_axis(value[i : i + 8, :], index, axis=1)
            for i in range(0, value.shape[0], 8)
        ]
        return jnp.concatenate(pieces, axis=0)

    signs = (1.0, 1.0, -1.0, -1.0)
    safe = (0.0, 1.0, 1.0, 0.0)
    turn = width - 1 - lane
    far, near = rows_n[base : base + 16, :], rows_s[base : base + 16, :]
    flipped = mirrored(far, turn)
    for m in range(4):
        metric[m, height:deep, :] = jnp.full((8, width), safe[m], jnp.float32)
        for k in range(RIM):
            at, fold = m * RIM + k, m * RIM + RIM - 1 - k
            metric[m, height + k : height + k + 1, :] = jnp.where(
                last, flipped[fold : fold + 1, :], far[at : at + 1, :]
            )
            metric[m, deep - RIM + k : deep - RIM + k + 1, :] = jnp.where(
                bottom, safe[m], near[at : at + 1, :]
            )
    made = factors(*[metric[m, height:deep, :] for m in range(4)])
    for m in range(6):
        table[m, height:deep, :] = made[m]
    for f in range(4):
        for k in range(RIM):
            at = (f * RIM + k) * levels
            fold = (f * RIM + RIM - 1 - k) * levels
            turned = signs[f] * mirrored(rows_n[fold : fold + levels, :], turn)
            state[f, :, height + k, :] = jnp.where(last, turned, rows_n[at : at + levels, :])
            state[f, :, deep - RIM + k, :] = rows_s[at : at + levels, :]
    rim = (row < RIM) | (row >= 8 - RIM)

    @pl.loop(0, levels)
    def _(level):
        wet = rim & (table[0, height:deep, :] > level.astype(jnp.float32))
        for f in range(4):
            state[f, level, height:deep, :] = jnp.where(wet, state[f, level, height:deep, :], 0.0)

    rows_in(*ends)
    side_far = strip_n[...]
    side_flipped = mirrored(side_far, group * 8 + jnp.where(within < 6, 5 - within, within))
    side_near = strip_s[...]
    for side in range(2):
        for f in range(5):
            if f == 4:
                fill = jnp.where((group == 1) | (group == 2), 1.0, 0.0)
            else:
                fill = jnp.zeros((8, width), jnp.float32)
            strips[side, f, height:deep, :] = fill
            for r in range(RIM):
                at = (side * 5 + f) * RIM + r
                fold = ((1 - side) * 5 + f) * RIM + RIM - 1 - r
                sign = 1.0 if f == 4 else signs[f]
                strips[side, f, height + r : height + r + 1, :] = jnp.where(
                    last, sign * side_flipped[fold : fold + 1, :], side_far[at : at + 1, :]
                )
                got = side_near[at : at + 1, :]
                if f == 4:
                    got = jnp.where(bottom, fill[0:1, :], got)
                strips[side, f, deep - RIM + r : deep - RIM + r + 1, :] = got
    side_tables(slice(height, deep))
    rows_sent(*main)
    rows_sent(*ends)


def substeps(
    state, table, sides, side_metric, mixing,
    y0, y1, y2, y3,
    second, third, result, sides_second, sides_third, link, store_sem,
):
    outs = (y0, y1, y2, y3)
    levels, deep, width = state.shape[1:]
    tiles = deep // 8
    lane = lanes((8, width))
    row = lax.broadcasted_iota(jnp.int32, (8, width), 0)
    group = lane // 8
    within = lane - group * 8

    def update(centre, easts, wests, norths, souths, factor, number, mix):
        bath, a2, b2, ah, bh, vo = factor
        wet = bath > number
        a2 = jnp.where(wet, a2, 0.0)
        b2 = jnp.where(wet, b2, 0.0)
        u, v = centre[2], centre[3]
        du, dv = u * ah, v * bh
        results = []
        for f in range(4):
            if f % 2 == 0:
                da, db = mix[f // 2] * a2, mix[f // 2] * b2
                ce, cw, cn, cs = da - du, da + du, db - dv, db + dv
                cc = 1.0 - 2.0 * (da + db)
            new = cc * centre[f] + (ce * easts[f] + cw * wests[f])
            new = new + (cn * norths[f] + cs * souths[f])
            if f == 2:
                new = new + vo * v
            if f == 3:
                new = new - vo * u
            results.append(new)
        return results

    def main_step(source, store, count):
        @pl.loop(0, levels)
        def _(level):
            number = level.astype(jnp.float32)
            mix = (mixing[0, level], mixing[1, level])
            for t in range(count):
                rows = slice(8 * t, 8 * t + 8)
                centre, easts, wests, norths, souths = [], [], [], [], []
                for f in range(4):
                    c = source[f, level, rows, :]
                    z = pltpu.roll(link[f, rows, :], width - 3 - 8 * (levels - 1) + 8 * level, 1)
                    centre.append(c)
                    easts.append(pltpu.roll(jnp.where(lane == 0, z, c), width - 1, 1))
                    wests.append(pltpu.roll(jnp.where(lane == width - 1, z, c), 1, 1))
                    if t < tiles - 1:
                        norths.append(source[f, level, 8 * t + 1 : 8 * t + 9, :])
                    else:
                        wrapped = pltpu.roll(source[f, level, 0:8, :], 7, 0)
                        norths.append(jnp.where(row == 7, wrapped, pltpu.roll(c, 7, 0)))
                    if t > 0:
                        souths.append(source[f, level, 8 * t - 1 : 8 * t + 7, :])
                    else:
                        wrapped = pltpu.roll(source[f, level, deep - 8 : deep, :], 1, 0)
                        souths.append(jnp.where(row == 0, wrapped, pltpu.roll(c, 1, 0)))
                factor = [table[m, rows, :] for m in range(6)]
                new = update(centre, easts, wests, norths, souths, factor, number, mix)
                for f in range(4):
                    store(f, level, t, new[f])

    def side_step(source, target):
        mix = (mixing[0, levels], mixing[1, levels])
        number = (levels - 1 - group).astype(jnp.float32)
        @pl.loop(0, tiles)
        def _(t):
            rows = pl.ds(pl.multiple_of(8 * t, 8), 8)
            prior = pl.ds(pl.multiple_of(lax.rem(t + tiles - 1, tiles) * 8, 8), 8)
            following = pl.ds(pl.multiple_of(lax.rem(t + 1, tiles) * 8, 8), 8)
            for side in range(2):
                centre = [source[side, f, rows, :] for f in range(4)]
                easts = [pltpu.roll(c, width - 1, 1) for c in centre]
                wests = [pltpu.roll(c, 1, 1) for c in centre]
                norths = [
                    jnp.where(
                        row == 7,
                        pltpu.roll(source[side, f, following, :], 7, 0),
                        pltpu.roll(centre[f], 7, 0),
                    )
                    for f in range(4)
                ]
                souths = [
                    jnp.where(
                        row == 0,
                        pltpu.roll(source[side, f, prior, :], 1, 0),
                        pltpu.roll(centre[f], 1, 0),
                    )
                    for f in range(4)
                ]
                factor = [side_metric[side, m, rows, :] for m in range(6)]
                new = update(centre, easts, wests, norths, souths, factor, number, mix)
                for f in range(4):
                    target[side, f, rows, :] = new[f]

    def join(source):
        @pl.loop(0, tiles)
        def _(t):
            rows = pl.ds(pl.multiple_of(t * 8, 8), 8)
            for f in range(4):
                link[f, rows, :] = jnp.where(within == 2, source[0, f, rows, :], source[1, f, rows, :])

    def into(buffer):
        def store(f, level, t, value):
            buffer[f, level, 8 * t : 8 * t + 8, :] = value
        return store

    def final(f, level, t, value):
        result[f, level, 8 * t : 8 * t + 8, :] = value

    join(sides)
    main_step(state, into(second), tiles)
    side_step(sides, sides_second)
    join(sides_second)
    main_step(second, into(third), tiles)
    side_step(sides_second, sides_third)
    join(sides_third)
    main_step(third, final, tiles - 1)
    stores = [
        pltpu.make_async_copy(result.at[f], outs[f], store_sem.at[f]) for f in range(4)
    ]
    for copy in stores:
        copy.start()
    for copy in stores:
        copy.wait()


def on_device(
    potential_heat_state,
    saltiness_anomaly,
    first_current_component,
    second_current_component,
    bathymetry_layer_total,
    westeast_cell_extent,
    southnorth_cell_extent,
    planetary_vorticity,
    scalar_mixing_factor,
    momentum_mixing_factor,
):
    fields = (potential_heat_state, saltiness_anomaly, first_current_component, second_current_component)
    metrics = (bathymetry_layer_total, westeast_cell_extent, southnorth_cell_extent, planetary_vorticity)
    levels, height, width = potential_heat_state.shape
    f32 = jnp.float32
    message = 4 * RIM * levels + 16
    deep = height + 8
    flat = (levels * height, width)
    vmem = pl.BlockSpec(memory_space=pltpu.VMEM)
    anywhere = pl.BlockSpec(memory_space=pltpu.HBM)
    laid = pl.pallas_call(
        exchange,
        out_shape=(
            pltpu.VMEM((4, levels, deep, width), f32),
            pltpu.VMEM((6, deep, width), f32),
            pltpu.VMEM((2, 4, deep, width), f32),
            pltpu.VMEM((2, 6, deep, width), f32),
            pltpu.VMEM((2, levels + 1, 8, width), f32),
        ),
        in_specs=[anywhere] * 10,
        out_specs=[vmem] * 5,
        scratch_shapes=[
            pltpu.SMEM((levels,), f32),
            pltpu.SMEM((levels,), f32),
            pltpu.VMEM((4,) + flat, f32),
            pltpu.VMEM((3, height, width), f32),
            pltpu.VMEM((height, width), jnp.int32),
            pltpu.VMEM((4, deep, width), f32),
            pltpu.VMEM((message, width), f32),
            pltpu.VMEM((message, width), f32),
            pltpu.VMEM((2, 5, deep, width), f32),
            pltpu.VMEM((32, width), f32),
            pltpu.VMEM((32, width), f32),
            pltpu.VMEM((message, width), f32),
            pltpu.VMEM((message, width), f32),
            pltpu.VMEM((5, height, width), f32),
            pltpu.VMEM((2, 3, height, width), f32),
            pltpu.VMEM((2, 3, height, width), f32),
            pltpu.VMEM((32, width), f32),
            pltpu.VMEM((32, width), f32),
            pltpu.SemaphoreType.DMA((6,)),
            pltpu.SemaphoreType.DMA((6,)),
            pltpu.SemaphoreType.DMA((10,)),
        ],
        compiler_params=pltpu.CompilerParams(
            collective_id=0, has_side_effects=True, vmem_limit_bytes=int(60.6 * 2**20)
        ),
        name="exchange",
    )(*[x.reshape(flat) for x in fields], *metrics, scalar_mixing_factor, momentum_mixing_factor)
    news = pl.pallas_call(
        substeps,
        out_shape=(jax.ShapeDtypeStruct((levels, height, width), f32),) * 4,
        in_specs=[vmem] * 5,
        out_specs=[anywhere] * 4,
        scratch_shapes=[
            pltpu.VMEM((4, levels, deep, width), f32),
            pltpu.VMEM((4, levels, deep, width), f32),
            pltpu.VMEM((4, levels, height, width), f32),
            pltpu.VMEM((2, 4, deep, width), f32),
            pltpu.VMEM((2, 4, deep, width), f32),
            pltpu.VMEM((4, deep, width), f32),
            pltpu.SemaphoreType.DMA((4,)),
        ],
        compiler_params=pltpu.CompilerParams(vmem_limit_bytes=32 * 2**20),
        name="substeps",
    )(*laid)
    return tuple(news)


def solution(mesh):
    state, plane = P(None, "lat", "lon"), P("lat", "lon")
    return jax.shard_map(
        on_device,
        mesh=mesh,
        in_specs=(state,) * 4 + (plane,) * 4 + (P(), P()),
        out_specs=(state,) * 4,
        check_vma=False,
    )
```

```python
import functools

import jax
import jax.numpy as jnp
from jax import lax
from jax.experimental import pallas as pl
from jax.experimental.pallas import tpu as pltpu
from jax.sharding import PartitionSpec as P

STEPS = 3
RIM = 3
time_step = 0.2

MESH = pl.DeviceIdType.MESH


def lanes(shape):
    return lax.broadcasted_iota(jnp.int32, shape, len(shape) - 1)


def factors(bath, we, sn, vo):
    a, b = 1.0 / we, 1.0 / sn
    return (
        bath, time_step * a * a, time_step * b * b,
        0.5 * time_step * a, 0.5 * time_step * b, time_step * vo,
    )


def exchange(
    x0, x1, x2, x3, bathy, wide, high, vort, tracer_mix, momentum_mix,
    state, table, sides, side_metric, mixing,
    factor_t, factor_m, field, whole, bath, metric,
    rows_n, rows_s, strips, strip_n, strip_s,
    out_n, out_s, packed, to_side, from_side, edge_n, edge_s,
    send_sem, recv_sem, load_sem,
):
    levels, width = state.shape[1], state.shape[3]
    height = wide.shape[0]
    deep = height + 8
    lat, lon = lax.axis_index("lat"), lax.axis_index("lon")
    lats, lons = lax.axis_size("lat"), lax.axis_size("lon")
    last, bottom = lat == lats - 1, lat == 0
    east = (lat, lax.rem(lon + 1, lons))
    west = (lat, lax.rem(lon + lons - 1, lons))
    north = (
        jnp.where(last, lat, lat + 1),
        jnp.where(last, lons - 1 - lon, lon),
    )
    south = (lat - 1, lon)

    loads = [
        pltpu.make_async_copy(x, field.at[f], load_sem.at[f]) for f, x in enumerate((x0, x1, x2, x3))
    ]
    loads.append(pltpu.make_async_copy(bathy, bath, load_sem.at[4]))
    loads += [
        pltpu.make_async_copy(x, whole.at[m], load_sem.at[5 + m]) for m, x in enumerate((wide, high, vort))
    ]
    loads += [
        pltpu.make_async_copy(tracer_mix, factor_t, load_sem.at[8]),
        pltpu.make_async_copy(momentum_mix, factor_m, load_sem.at[9]),
    ]
    for load in loads:
        load.start()

    barrier = pltpu.get_barrier_semaphore()
    for peer in (east, west, north):
        pl.semaphore_signal(barrier, inc=1, device_id=peer, device_id_type=MESH)

    @pl.when(lat > 0)
    def _():
        pl.semaphore_signal(barrier, inc=1, device_id=south, device_id_type=MESH)

    lane = lanes((8, width))
    row = lax.broadcasted_iota(jnp.int32, (8, width), 0)
    group = lane // 8
    within = lane - group * 8

    def pack(pair, tile):
        start = pl.multiple_of(tile * 8, 8)
        rows = pl.ds(start, 8)
        cols = []
        for f in (2 * pair, 2 * pair + 1):
            acc = pltpu.roll(field[f, rows, :], 8 * (levels - 1) + RIM, 1)
            for level in range(1, levels):
                spot = levels - 1 - level
                at = pl.ds(pl.multiple_of(start + level * height, 8), 8)
                acc = jnp.where(group == spot, pltpu.roll(field[f, at, :], 8 * spot + RIM, 1), acc)
            packed[f, rows, :] = acc
            cols.append(acc)
        if pair == 0:
            acc = jnp.zeros((8, width), jnp.float32)
            raw = (bath[rows, :].astype(jnp.float32), whole[0, rows, :], whole[1, rows, :], whole[2, rows, :])
            for m in range(4):
                metric[m, rows, :] = raw[m]
                acc = jnp.where(group == m, pltpu.roll(raw[m], 8 * m + RIM, 1), acc)
            packed[4, rows, :] = acc
            extra_w = pltpu.roll(acc, 3, 1)
            extra_e = jnp.where(within == 3, extra_w, pltpu.roll(acc, 6, 1))
        else:
            extra_e = extra_w = pltpu.roll(packed[4, rows, :], 1, 1)
        one, two = cols
        to_side[0, pair, rows, :] = jnp.where(
            within < 3, one, jnp.where((within == 3) | (within == 7), extra_e, pltpu.roll(two, 4, 1))
        )
        to_side[1, pair, rows, :] = jnp.where(
            within < 3, pltpu.roll(two, width - 3, 1), jnp.where(within < 6, one, extra_w)
        )

    for at in (0, 1, 4, 5, 6, 7):
        loads[at].wait()

    @pl.loop(0, height // 8)
    def _(tile):
        pack(0, tile)

    @pl.when(lat > 0)
    def _():
        pl.semaphore_wait(barrier, 4)

    @pl.when(lat == 0)
    def _():
        pl.semaphore_wait(barrier, 3)

    def remote(src, dst, which, arrive, peer):
        return pltpu.make_async_remote_copy(
            src_ref=src, dst_ref=dst, send_sem=send_sem.at[which], recv_sem=recv_sem.at[arrive],
            device_id=peer, device_id_type=MESH,
        )

    across = []
    for pair in range(2):
        across.append(remote(to_side.at[0, pair], from_side.at[0, pair], 6 * pair, 6 * pair, east))
        across.append(remote(to_side.at[1, pair], from_side.at[1, pair], 6 * pair + 1, 6 * pair + 1, west))
    across[0].start()
    across[1].start()
    for at in (2, 3, 8, 9):
        loads[at].wait()

    @pl.loop(0, height // 8)
    def _(tile):
        pack(1, tile)

    across[2].start()
    across[3].start()

    def column(f, r, half):
        return field[f, pl.ds(r + half * 8 * height, 8, stride=height), :]

    for f in range(4):
        for r in range(RIM):
            at = (f * RIM + r) * levels
            for half in range(levels // 8):
                rows = slice(at + 8 * half, at + 8 * half + 8)
                out_s[rows, :] = column(f, r, half)
                out_n[rows, :] = column(f, height - RIM + r, half)
    base = 4 * RIM * levels
    out_s[base : base + 16, :] = jnp.zeros((16, width), jnp.float32)
    out_n[base : base + 16, :] = jnp.zeros((16, width), jnp.float32)
    for m in range(4):
        out_s[base + m * RIM : base + (m + 1) * RIM, :] = metric[m, 0:RIM, :]
        out_n[base + m * RIM : base + (m + 1) * RIM, :] = metric[m, height - RIM : height, :]

    def rows_out(to_n, to_s, recv_n, recv_s, first):
        up = remote(to_n, recv_s, first, first, north)
        fold = remote(to_n, recv_n, first, first + 1, north)
        down = remote(to_s, recv_n, first + 1, first + 1, south)

        @pl.when(last)
        def _():
            fold.start()

        @pl.when(lat < lats - 1)
        def _():
            up.start()

        @pl.when(lat > 0)
        def _():
            down.start()

        return up, down

    def rows_in(up, down):
        down.wait_recv()

        @pl.when(lat > 0)
        def _():
            up.wait_recv()

    def rows_sent(up, down):
        up.wait_send()

        @pl.when(lat > 0)
        def _():
            down.wait_send()

    @pl.when(lat == 0)
    def _():
        rows_s[...] = jnp.zeros(rows_s.shape, jnp.float32)
        strip_s[...] = jnp.zeros(strip_s.shape, jnp.float32)

    main = rows_out(out_n, out_s, rows_n, rows_s, 2)

    @pl.loop(0, height // 8)
    def _(tile):
        rows = pl.ds(pl.multiple_of(tile * 8, 8), 8)
        made = factors(*[metric[m, rows, :] for m in range(4)])
        for m in range(6):
            table[m, rows, :] = made[m]

    for copy in across:
        copy.wait_recv()

    @pl.loop(0, height // 8)
    def _(tile):
        rows = pl.ds(pl.multiple_of(tile * 8, 8), 8)
        for f in range(4):
            own = packed[f, rows, :]
            got_w = from_side[0, f // 2, rows, :]
            got_e = from_side[1, f // 2, rows, :]
            if f % 2 == 1:
                got_w = pltpu.roll(got_w, width - 4, 1)
                got_e = pltpu.roll(got_e, 3, 1)
            strips[0, f, rows, :] = jnp.where(within < RIM, got_w, own)
            strips[1, f, rows, :] = jnp.where(within < RIM, own, got_e)
        own = packed[4, rows, :]
        first, second = from_side[0, 0, rows, :], from_side[0, 1, rows, :]
        got_w = jnp.where(
            within == 0,
            pltpu.roll(first, width - 3, 1),
            jnp.where(within == 1, pltpu.roll(first, width - 6, 1), pltpu.roll(second, width - 1, 1)),
        )
        first, second = from_side[1, 0, rows, :], from_side[1, 1, rows, :]
        got_e = jnp.where(within < 5, pltpu.roll(first, width - 3, 1), pltpu.roll(second, width - 1, 1))
        strips[0, 4, rows, :] = jnp.where(within < RIM, got_w, own)
        strips[1, 4, rows, :] = jnp.where((within < RIM) | (within > 5), own, got_e)

    edge_n[30:32, :] = jnp.zeros((2, width), jnp.float32)
    edge_s[30:32, :] = jnp.zeros((2, width), jnp.float32)
    for side in range(2):
        for f in range(5):
            at = (side * 5 + f) * RIM
            edge_s[at : at + RIM, :] = strips[side, f, 0:RIM, :]
            edge_n[at : at + RIM, :] = strips[side, f, height - RIM : height, :]
    ends = rows_out(edge_n, edge_s, strip_n, strip_s, 4)

    @pl.loop(0, levels)
    def _(level):
        number = level.astype(jnp.float32)
        for t in range(height // 8):
            wet = table[0, 8 * t : 8 * t + 8, :] > number
            at = pl.ds(pl.multiple_of(level * height + 8 * t, 8), 8)
            for f in range(4):
                state[f, level, 8 * t : 8 * t + 8, :] = jnp.where(wet, field[f, at, :], 0.0)

    for k, mix in enumerate((factor_t, factor_m)):
        spread = jnp.zeros((8, width), jnp.float32)
        for level in range(levels):
            spread = jnp.where(group == levels - 1 - level, mix[level], spread)
            mixing[k, level] = jnp.full((8, width), mix[level], jnp.float32)
        mixing[k, levels] = spread

    def side_tables(rows):
        for side in range(2):
            mixed = strips[side, 4, rows, :]
            spread = []
            for m in range(4):
                value = jnp.where(group == m, mixed, 0.0)
                for hop in (8, 16, 32, 64):
                    value = value + pltpu.roll(value, hop, 1)
                spread.append(value)
            made = factors(*spread)
            for m in range(6):
                side_metric[side, m, rows, :] = made[m]
            wet = made[0] > (levels - 1 - group).astype(jnp.float32)
            for f in range(4):
                sides[side, f, rows, :] = jnp.where(wet, strips[side, f, rows, :], 0.0)

    @pl.loop(0, height // 8)
    def _(tile):
        side_tables(pl.ds(pl.multiple_of(tile * 8, 8), 8))

    for copy in across:
        copy.wait_send()
    rows_in(*main)

    def mirrored(value, index):
        pieces = [
            jnp.take_along_axis(value[i : i + 8, :], index, axis=1)
            for i in range(0, value.shape[0], 8)
        ]
        return jnp.concatenate(pieces, axis=0)

    signs = (1.0, 1.0, -1.0, -1.0)
    safe = (0.0, 1.0, 1.0, 0.0)
    turn = width - 1 - lane
    far, near = rows_n[base : base + 16, :], rows_s[base : base + 16, :]
    flipped = mirrored(far, turn)
    for m in range(4):
        metric[m, height:deep, :] = jnp.full((8, width), safe[m], jnp.float32)
        for k in range(RIM):
            at, fold = m * RIM + k, m * RIM + RIM - 1 - k
            metric[m, height + k : height + k + 1, :] = jnp.where(
                last, flipped[fold : fold + 1, :], far[at : at + 1, :]
            )
            metric[m, deep - RIM + k : deep - RIM + k + 1, :] = jnp.where(
                bottom, safe[m], near[at : at + 1, :]
            )
    made = factors(*[metric[m, height:deep, :] for m in range(4)])
    for m in range(6):
        table[m, height:deep, :] = made[m]
    for f in range(4):
        for k in range(RIM):
            at = (f * RIM + k) * levels
            fold = (f * RIM + RIM - 1 - k) * levels
            turned = signs[f] * mirrored(rows_n[fold : fold + levels, :], turn)
            state[f, :, height + k, :] = jnp.where(last, turned, rows_n[at : at + levels, :])
            state[f, :, deep - RIM + k, :] = rows_s[at : at + levels, :]
    rim = (row < RIM) | (row >= 8 - RIM)

    @pl.loop(0, levels)
    def _(level):
        wet = rim & (table[0, height:deep, :] > level.astype(jnp.float32))
        for f in range(4):
            state[f, level, height:deep, :] = jnp.where(wet, state[f, level, height:deep, :], 0.0)

    rows_in(*ends)
    side_far = strip_n[...]
    side_flipped = mirrored(side_far, group * 8 + jnp.where(within < 6, 5 - within, within))
    side_near = strip_s[...]
    for side in range(2):
        for f in range(5):
            if f == 4:
                fill = jnp.where((group == 1) | (group == 2), 1.0, 0.0)
            else:
                fill = jnp.zeros((8, width), jnp.float32)
            strips[side, f, height:deep, :] = fill
            for r in range(RIM):
                at = (side * 5 + f) * RIM + r
                fold = ((1 - side) * 5 + f) * RIM + RIM - 1 - r
                sign = 1.0 if f == 4 else signs[f]
                strips[side, f, height + r : height + r + 1, :] = jnp.where(
                    last, sign * side_flipped[fold : fold + 1, :], side_far[at : at + 1, :]
                )
                got = side_near[at : at + 1, :]
                if f == 4:
                    got = jnp.where(bottom, fill[0:1, :], got)
                strips[side, f, deep - RIM + r : deep - RIM + r + 1, :] = got
    side_tables(slice(height, deep))
    rows_sent(*main)
    rows_sent(*ends)


def substeps(
    state, table, sides, side_metric, mixing,
    y0, y1, y2, y3,
    second, third, result, sides_second, sides_third, link, store_sem,
):
    outs = (y0, y1, y2, y3)
    levels, deep, width = state.shape[1:]
    tiles = deep // 8
    lane = lanes((8, width))
    row = lax.broadcasted_iota(jnp.int32, (8, width), 0)
    group = lane // 8
    within = lane - group * 8

    def update(centre, easts, wests, norths, souths, factor, number, mix):
        bath, a2, b2, ah, bh, vo = factor
        wet = bath > number
        a2 = jnp.where(wet, a2, 0.0)
        b2 = jnp.where(wet, b2, 0.0)
        u, v = centre[2], centre[3]
        du, dv = u * ah, v * bh
        results = []
        for f in range(4):
            if f % 2 == 0:
                da, db = mix[f // 2] * a2, mix[f // 2] * b2
                ce, cw, cn, cs = da - du, da + du, db - dv, db + dv
                cc = 1.0 - 2.0 * (da + db)
            new = cc * centre[f] + (ce * easts[f] + cw * wests[f])
            new = new + (cn * norths[f] + cs * souths[f])
            if f == 2:
                new = new + vo * v
            if f == 3:
                new = new - vo * u
            results.append(new)
        return results

    def main_step(source, store, count, after=None):
        @pl.loop(0, levels)
        def _(level):
            number = level.astype(jnp.float32)
            mix = (mixing[0, level], mixing[1, level])
            for t in range(count):
                rows = slice(8 * t, 8 * t + 8)
                centre, easts, wests, norths, souths = [], [], [], [], []
                for f in range(4):
                    c = source[f, level, rows, :]
                    z = pltpu.roll(link[f, rows, :], width - 3 - 8 * (levels - 1) + 8 * level, 1)
                    centre.append(c)
                    easts.append(pltpu.roll(jnp.where(lane == 0, z, c), width - 1, 1))
                    wests.append(pltpu.roll(jnp.where(lane == width - 1, z, c), 1, 1))
                    if t < tiles - 1:
                        norths.append(source[f, level, 8 * t + 1 : 8 * t + 9, :])
                    else:
                        wrapped = pltpu.roll(source[f, level, 0:8, :], 7, 0)
                        norths.append(jnp.where(row == 7, wrapped, pltpu.roll(c, 7, 0)))
                    if t > 0:
                        souths.append(source[f, level, 8 * t - 1 : 8 * t + 7, :])
                    else:
                        wrapped = pltpu.roll(source[f, level, deep - 8 : deep, :], 1, 0)
                        souths.append(jnp.where(row == 0, wrapped, pltpu.roll(c, 1, 0)))
                factor = [table[m, rows, :] for m in range(6)]
                new = update(centre, easts, wests, norths, souths, factor, number, mix)
                for f in range(4):
                    store(f, level, t, new[f])
            if after is not None:
                after(level)

    def side_step(source, target):
        mix = (mixing[0, levels], mixing[1, levels])
        number = (levels - 1 - group).astype(jnp.float32)
        @pl.loop(0, tiles)
        def _(t):
            rows = pl.ds(pl.multiple_of(8 * t, 8), 8)
            prior = pl.ds(pl.multiple_of(lax.rem(t + tiles - 1, tiles) * 8, 8), 8)
            following = pl.ds(pl.multiple_of(lax.rem(t + 1, tiles) * 8, 8), 8)
            for side in range(2):
                centre = [source[side, f, rows, :] for f in range(4)]
                easts = [pltpu.roll(c, width - 1, 1) for c in centre]
                wests = [pltpu.roll(c, 1, 1) for c in centre]
                norths = [
                    jnp.where(
                        row == 7,
                        pltpu.roll(source[side, f, following, :], 7, 0),
                        pltpu.roll(centre[f], 7, 0),
                    )
                    for f in range(4)
                ]
                souths = [
                    jnp.where(
                        row == 0,
                        pltpu.roll(source[side, f, prior, :], 1, 0),
                        pltpu.roll(centre[f], 1, 0),
                    )
                    for f in range(4)
                ]
                factor = [side_metric[side, m, rows, :] for m in range(6)]
                new = update(centre, easts, wests, norths, souths, factor, number, mix)
                for f in range(4):
                    target[side, f, rows, :] = new[f]

    def join(source):
        @pl.loop(0, tiles)
        def _(t):
            rows = pl.ds(pl.multiple_of(t * 8, 8), 8)
            for f in range(4):
                link[f, rows, :] = jnp.where(within == 2, source[0, f, rows, :], source[1, f, rows, :])

    def into(buffer):
        def store(f, level, t, value):
            buffer[f, level, 8 * t : 8 * t + 8, :] = value
        return store

    def final(f, level, t, value):
        result[f, level, 8 * t : 8 * t + 8, :] = value

    join(sides)
    main_step(state, into(second), tiles)
    side_step(sides, sides_second)
    join(sides_second)
    main_step(second, into(third), tiles)
    side_step(sides_second, sides_third)
    join(sides_third)

    def leave(level):
        for f in range(4):
            pltpu.make_async_copy(result.at[f, level], outs[f].at[level], store_sem.at[f]).start()

    main_step(third, final, tiles - 1, leave)
    for f in range(4):
        pltpu.make_async_copy(result.at[f], outs[f], store_sem.at[f]).wait()


def on_device(
    potential_heat_state,
    saltiness_anomaly,
    first_current_component,
    second_current_component,
    bathymetry_layer_total,
    westeast_cell_extent,
    southnorth_cell_extent,
    planetary_vorticity,
    scalar_mixing_factor,
    momentum_mixing_factor,
):
    fields = (potential_heat_state, saltiness_anomaly, first_current_component, second_current_component)
    metrics = (bathymetry_layer_total, westeast_cell_extent, southnorth_cell_extent, planetary_vorticity)
    levels, height, width = potential_heat_state.shape
    f32 = jnp.float32
    message = 4 * RIM * levels + 16
    deep = height + 8
    flat = (levels * height, width)
    vmem = pl.BlockSpec(memory_space=pltpu.VMEM)
    anywhere = pl.BlockSpec(memory_space=pltpu.HBM)
    laid = pl.pallas_call(
        exchange,
        out_shape=(
            pltpu.VMEM((4, levels, deep, width), f32),
            pltpu.VMEM((6, deep, width), f32),
            pltpu.VMEM((2, 4, deep, width), f32),
            pltpu.VMEM((2, 6, deep, width), f32),
            pltpu.VMEM((2, levels + 1, 8, width), f32),
        ),
        in_specs=[anywhere] * 10,
        out_specs=[vmem] * 5,
        scratch_shapes=[
            pltpu.SMEM((levels,), f32),
            pltpu.SMEM((levels,), f32),
            pltpu.VMEM((4,) + flat, f32),
            pltpu.VMEM((3, height, width), f32),
            pltpu.VMEM((height, width), jnp.int32),
            pltpu.VMEM((4, deep, width), f32),
            pltpu.VMEM((message, width), f32),
            pltpu.VMEM((message, width), f32),
            pltpu.VMEM((2, 5, deep, width), f32),
            pltpu.VMEM((32, width), f32),
            pltpu.VMEM((32, width), f32),
            pltpu.VMEM((message, width), f32),
            pltpu.VMEM((message, width), f32),
            pltpu.VMEM((5, height, width), f32),
            pltpu.VMEM((2, 2, height, width), f32),
            pltpu.VMEM((2, 2, height, width), f32),
            pltpu.VMEM((32, width), f32),
            pltpu.VMEM((32, width), f32),
            pltpu.SemaphoreType.DMA((8,)),
            pltpu.SemaphoreType.DMA((8,)),
            pltpu.SemaphoreType.DMA((10,)),
        ],
        compiler_params=pltpu.CompilerParams(
            collective_id=0, has_side_effects=True, vmem_limit_bytes=int(60.6 * 2**20)
        ),
        name="exchange",
    )(*[x.reshape(flat) for x in fields], *metrics, scalar_mixing_factor, momentum_mixing_factor)
    news = pl.pallas_call(
        substeps,
        out_shape=(jax.ShapeDtypeStruct((levels, height, width), f32),) * 4,
        in_specs=[vmem] * 5,
        out_specs=[anywhere] * 4,
        scratch_shapes=[
            pltpu.VMEM((4, levels, deep, width), f32),
            pltpu.VMEM((4, levels, deep, width), f32),
            pltpu.VMEM((4, levels, height, width), f32),
            pltpu.VMEM((2, 4, deep, width), f32),
            pltpu.VMEM((2, 4, deep, width), f32),
            pltpu.VMEM((4, deep, width), f32),
            pltpu.SemaphoreType.DMA((4,)),
        ],
        compiler_params=pltpu.CompilerParams(vmem_limit_bytes=32 * 2**20),
        name="substeps",
    )(*laid)
    return tuple(news)


def solution(mesh):
    state, plane = P(None, "lat", "lon"), P("lat", "lon")
    return jax.shard_map(
        on_device,
        mesh=mesh,
        in_specs=(state,) * 4 + (plane,) * 4 + (P(), P()),
        out_specs=(state,) * 4,
        check_vma=False,
    )
```

```python
import functools

import jax
import jax.numpy as jnp
from jax import lax
from jax.experimental import pallas as pl
from jax.experimental.pallas import tpu as pltpu
from jax.sharding import PartitionSpec as P

STEPS = 3
RIM = 3
time_step = 0.2

MESH = pl.DeviceIdType.MESH


def lanes(shape):
    return lax.broadcasted_iota(jnp.int32, shape, len(shape) - 1)


def factors(bath, we, sn, vo):
    a, b = 1.0 / we, 1.0 / sn
    return (
        bath, time_step * a * a, time_step * b * b,
        0.5 * time_step * a, 0.5 * time_step * b, time_step * vo,
    )


def exchange(
    x0, x1, x2, x3, bathy, wide, high, vort, tracer_mix, momentum_mix,
    state, table, sides, side_metric, mixing,
    factor_t, factor_m, field, whole, bath, metric,
    rows_n, rows_s, strips, strip_n, strip_s,
    out_n, out_s, packed, to_side, from_side, edge_n, edge_s,
    send_sem, recv_sem, load_sem,
):
    levels, width = state.shape[1], state.shape[3]
    height = wide.shape[0]
    deep = height + 8
    lat, lon = lax.axis_index("lat"), lax.axis_index("lon")
    lats, lons = lax.axis_size("lat"), lax.axis_size("lon")
    last, bottom = lat == lats - 1, lat == 0
    east = (lat, lax.rem(lon + 1, lons))
    west = (lat, lax.rem(lon + lons - 1, lons))
    north = (
        jnp.where(last, lat, lat + 1),
        jnp.where(last, lons - 1 - lon, lon),
    )
    south = (lat - 1, lon)

    loads = [
        pltpu.make_async_copy(x, field.at[f], load_sem.at[f]) for f, x in enumerate((x0, x1, x2, x3))
    ]
    loads.append(pltpu.make_async_copy(bathy, bath, load_sem.at[4]))
    loads += [
        pltpu.make_async_copy(x, whole.at[m], load_sem.at[5 + m]) for m, x in enumerate((wide, high, vort))
    ]
    loads += [
        pltpu.make_async_copy(tracer_mix, factor_t, load_sem.at[8]),
        pltpu.make_async_copy(momentum_mix, factor_m, load_sem.at[9]),
    ]
    for load in loads:
        load.start()

    barrier = pltpu.get_barrier_semaphore()
    for peer in (east, west, north):
        pl.semaphore_signal(barrier, inc=1, device_id=peer, device_id_type=MESH)

    @pl.when(lat > 0)
    def _():
        pl.semaphore_signal(barrier, inc=1, device_id=south, device_id_type=MESH)

    lane = lanes((8, width))
    row = lax.broadcasted_iota(jnp.int32, (8, width), 0)
    group = lane // 8
    within = lane - group * 8

    def pack(pair, tile):
        start = pl.multiple_of(tile * 8, 8)
        rows = pl.ds(start, 8)
        cols = []
        for f in (2 * pair, 2 * pair + 1):
            acc = pltpu.roll(field[f, rows, :], 8 * (levels - 1) + RIM, 1)
            for level in range(1, levels):
                spot = levels - 1 - level
                at = pl.ds(pl.multiple_of(start + level * height, 8), 8)
                acc = jnp.where(group == spot, pltpu.roll(field[f, at, :], 8 * spot + RIM, 1), acc)
            packed[f, rows, :] = acc
            cols.append(acc)
        if pair == 0:
            acc = jnp.zeros((8, width), jnp.float32)
            raw = (bath[rows, :].astype(jnp.float32), whole[0, rows, :], whole[1, rows, :], whole[2, rows, :])
            for m in range(4):
                metric[m, rows, :] = raw[m]
                acc = jnp.where(group == m, pltpu.roll(raw[m], 8 * m + RIM, 1), acc)
            packed[4, rows, :] = acc
            extra_w = pltpu.roll(acc, 3, 1)
            extra_e = jnp.where(within == 3, extra_w, pltpu.roll(acc, 6, 1))
        else:
            extra_e = extra_w = pltpu.roll(packed[4, rows, :], 1, 1)
        one, two = cols
        to_side[0, pair, rows, :] = jnp.where(
            within < 3, one, jnp.where((within == 3) | (within == 7), extra_e, pltpu.roll(two, 4, 1))
        )
        to_side[1, pair, rows, :] = jnp.where(
            within < 3, pltpu.roll(two, width - 3, 1), jnp.where(within < 6, one, extra_w)
        )

    for at in (0, 1, 4, 5, 6, 7):
        loads[at].wait()

    @pl.loop(0, height // 8)
    def _(tile):
        pack(0, tile)

    @pl.when(lat > 0)
    def _():
        pl.semaphore_wait(barrier, 4)

    @pl.when(lat == 0)
    def _():
        pl.semaphore_wait(barrier, 3)

    def remote(src, dst, which, arrive, peer):
        return pltpu.make_async_remote_copy(
            src_ref=src, dst_ref=dst, send_sem=send_sem.at[which], recv_sem=recv_sem.at[arrive],
            device_id=peer, device_id_type=MESH,
        )

    across = []
    for pair in range(2):
        across.append(remote(to_side.at[0, pair], from_side.at[0, pair], 6 * pair, 6 * pair, east))
        across.append(remote(to_side.at[1, pair], from_side.at[1, pair], 6 * pair + 1, 6 * pair + 1, west))
    across[0].start()
    across[1].start()
    for at in (2, 3, 8, 9):
        loads[at].wait()

    @pl.loop(0, height // 8)
    def _(tile):
        pack(1, tile)

    across[2].start()
    across[3].start()

    def column(f, r, half):
        return field[f, pl.ds(r + half * 8 * height, 8, stride=height), :]

    for f in range(4):
        for r in range(RIM):
            at = (f * RIM + r) * levels
            for half in range(levels // 8):
                rows = slice(at + 8 * half, at + 8 * half + 8)
                out_s[rows, :] = column(f, r, half)
                out_n[rows, :] = column(f, height - RIM + r, half)
    base = 4 * RIM * levels
    out_s[base : base + 16, :] = jnp.zeros((16, width), jnp.float32)
    out_n[base : base + 16, :] = jnp.zeros((16, width), jnp.float32)
    for m in range(4):
        out_s[base + m * RIM : base + (m + 1) * RIM, :] = metric[m, 0:RIM, :]
        out_n[base + m * RIM : base + (m + 1) * RIM, :] = metric[m, height - RIM : height, :]

    def rows_out(to_n, to_s, recv_n, recv_s, first):
        up = remote(to_n, recv_s, first, first, north)
        fold = remote(to_n, recv_n, first, first + 1, north)
        down = remote(to_s, recv_n, first + 1, first + 1, south)

        @pl.when(last)
        def _():
            fold.start()

        @pl.when(lat < lats - 1)
        def _():
            up.start()

        @pl.when(lat > 0)
        def _():
            down.start()

        return up, down

    def rows_in(up, down):
        down.wait_recv()

        @pl.when(lat > 0)
        def _():
            up.wait_recv()

    def rows_sent(up, down):
        up.wait_send()

        @pl.when(lat > 0)
        def _():
            down.wait_send()

    @pl.when(lat == 0)
    def _():
        rows_s[...] = jnp.zeros(rows_s.shape, jnp.float32)
        strip_s[...] = jnp.zeros(strip_s.shape, jnp.float32)

    main = rows_out(out_n, out_s, rows_n, rows_s, 2)

    @pl.loop(0, height // 8)
    def _(tile):
        rows = pl.ds(pl.multiple_of(tile * 8, 8), 8)
        made = factors(*[metric[m, rows, :] for m in range(4)])
        for m in range(6):
            table[m, rows, :] = made[m]

    for copy in across:
        copy.wait_recv()

    @pl.loop(0, height // 8)
    def _(tile):
        rows = pl.ds(pl.multiple_of(tile * 8, 8), 8)
        for f in range(4):
            own = packed[f, rows, :]
            got_w = from_side[0, f // 2, rows, :]
            got_e = from_side[1, f // 2, rows, :]
            if f % 2 == 1:
                got_w = pltpu.roll(got_w, width - 4, 1)
                got_e = pltpu.roll(got_e, 3, 1)
            strips[0, f, rows, :] = jnp.where(within < RIM, got_w, own)
            strips[1, f, rows, :] = jnp.where(within < RIM, own, got_e)
        own = packed[4, rows, :]
        first, second = from_side[0, 0, rows, :], from_side[0, 1, rows, :]
        got_w = jnp.where(
            within == 0,
            pltpu.roll(first, width - 3, 1),
            jnp.where(within == 1, pltpu.roll(first, width - 6, 1), pltpu.roll(second, width - 1, 1)),
        )
        first, second = from_side[1, 0, rows, :], from_side[1, 1, rows, :]
        got_e = jnp.where(within < 5, pltpu.roll(first, width - 3, 1), pltpu.roll(second, width - 1, 1))
        strips[0, 4, rows, :] = jnp.where(within < RIM, got_w, own)
        strips[1, 4, rows, :] = jnp.where((within < RIM) | (within > 5), own, got_e)

    edge_n[30:32, :] = jnp.zeros((2, width), jnp.float32)
    edge_s[30:32, :] = jnp.zeros((2, width), jnp.float32)
    for side in range(2):
        for f in range(5):
            at = (side * 5 + f) * RIM
            edge_s[at : at + RIM, :] = strips[side, f, 0:RIM, :]
            edge_n[at : at + RIM, :] = strips[side, f, height - RIM : height, :]
    ends = rows_out(edge_n, edge_s, strip_n, strip_s, 4)

    @pl.loop(0, levels)
    def _(level):
        number = level.astype(jnp.float32)
        for t in range(height // 8):
            wet = table[0, 8 * t : 8 * t + 8, :] > number
            at = pl.ds(pl.multiple_of(level * height + 8 * t, 8), 8)
            for f in range(4):
                state[f, level, 8 * t : 8 * t + 8, :] = jnp.where(wet, field[f, at, :], 0.0)

    for k, mix in enumerate((factor_t, factor_m)):
        spread = jnp.zeros((8, width), jnp.float32)
        for level in range(levels):
            spread = jnp.where(group == levels - 1 - level, mix[level], spread)
            mixing[k, level] = jnp.full((8, width), mix[level], jnp.float32)
        mixing[k, levels] = spread

    def side_tables(rows):
        for side in range(2):
            mixed = strips[side, 4, rows, :]
            spread = []
            for m in range(4):
                value = jnp.where(group == m, mixed, 0.0)
                for hop in (8, 16, 32, 64):
                    value = value + pltpu.roll(value, hop, 1)
                spread.append(value)
            made = factors(*spread)
            for m in range(6):
                side_metric[side, m, rows, :] = made[m]
            wet = made[0] > (levels - 1 - group).astype(jnp.float32)
            for f in range(4):
                sides[side, f, rows, :] = jnp.where(wet, strips[side, f, rows, :], 0.0)

    @pl.loop(0, height // 8)
    def _(tile):
        side_tables(pl.ds(pl.multiple_of(tile * 8, 8), 8))

    for copy in across:
        copy.wait_send()
    rows_in(*main)

    def mirrored(value, index):
        pieces = [
            jnp.take_along_axis(value[i : i + 8, :], index, axis=1)
            for i in range(0, value.shape[0], 8)
        ]
        return jnp.concatenate(pieces, axis=0)

    signs = (1.0, 1.0, -1.0, -1.0)
    safe = (0.0, 1.0, 1.0, 0.0)
    turn = width - 1 - lane
    far, near = rows_n[base : base + 16, :], rows_s[base : base + 16, :]
    flipped = mirrored(far, turn)
    for m in range(4):
        metric[m, height:deep, :] = jnp.full((8, width), safe[m], jnp.float32)
        for k in range(RIM):
            at, fold = m * RIM + k, m * RIM + RIM - 1 - k
            metric[m, height + k : height + k + 1, :] = jnp.where(
                last, flipped[fold : fold + 1, :], far[at : at + 1, :]
            )
            metric[m, deep - RIM + k : deep - RIM + k + 1, :] = jnp.where(
                bottom, safe[m], near[at : at + 1, :]
            )
    made = factors(*[metric[m, height:deep, :] for m in range(4)])
    for m in range(6):
        table[m, height:deep, :] = made[m]
    for f in range(4):
        for k in range(RIM):
            at = (f * RIM + k) * levels
            fold = (f * RIM + RIM - 1 - k) * levels
            turned = signs[f] * mirrored(rows_n[fold : fold + levels, :], turn)
            state[f, :, height + k, :] = jnp.where(last, turned, rows_n[at : at + levels, :])
            state[f, :, deep - RIM + k, :] = rows_s[at : at + levels, :]
    rim = (row < RIM) | (row >= 8 - RIM)

    @pl.loop(0, levels)
    def _(level):
        wet = rim & (table[0, height:deep, :] > level.astype(jnp.float32))
        for f in range(4):
            state[f, level, height:deep, :] = jnp.where(wet, state[f, level, height:deep, :], 0.0)

    rows_in(*ends)
    side_far = strip_n[...]
    side_flipped = mirrored(side_far, group * 8 + jnp.where(within < 6, 5 - within, within))
    side_near = strip_s[...]
    for side in range(2):
        for f in range(5):
            if f == 4:
                fill = jnp.where((group == 1) | (group == 2), 1.0, 0.0)
            else:
                fill = jnp.zeros((8, width), jnp.float32)
            strips[side, f, height:deep, :] = fill
            for r in range(RIM):
                at = (side * 5 + f) * RIM + r
                fold = ((1 - side) * 5 + f) * RIM + RIM - 1 - r
                sign = 1.0 if f == 4 else signs[f]
                strips[side, f, height + r : height + r + 1, :] = jnp.where(
                    last, sign * side_flipped[fold : fold + 1, :], side_far[at : at + 1, :]
                )
                got = side_near[at : at + 1, :]
                if f == 4:
                    got = jnp.where(bottom, fill[0:1, :], got)
                strips[side, f, deep - RIM + r : deep - RIM + r + 1, :] = got
    side_tables(slice(height, deep))
    rows_sent(*main)
    rows_sent(*ends)


def substeps(
    state, table, sides, side_metric, mixing,
    y0, y1, y2, y3,
    second, third, result, sides_second, sides_third, link, store_sem,
):
    outs = (y0, y1, y2, y3)
    levels, deep, width = state.shape[1:]
    tiles = deep // 8
    lane = lanes((8, width))
    row = lax.broadcasted_iota(jnp.int32, (8, width), 0)
    group = lane // 8
    within = lane - group * 8

    def update(centre, easts, wests, norths, souths, factor, number, mix):
        bath, a2, b2, ah, bh, vo = factor
        wet = bath > number
        a2 = jnp.where(wet, a2, 0.0)
        b2 = jnp.where(wet, b2, 0.0)
        u, v = centre[2], centre[3]
        du, dv = u * ah, v * bh
        results = []
        for f in range(4):
            if f % 2 == 0:
                da, db = mix[f // 2] * a2, mix[f // 2] * b2
                ce, cw, cn, cs = da - du, da + du, db - dv, db + dv
                cc = 1.0 - 2.0 * (da + db)
            new = cc * centre[f] + (ce * easts[f] + cw * wests[f])
            new = new + (cn * norths[f] + cs * souths[f])
            if f == 2:
                new = new + vo * v
            if f == 3:
                new = new - vo * u
            results.append(new)
        return results

    def main_step(source, store, count, after=None):
        flat = source.reshape(4, levels * deep, width)

        @pl.loop(0, levels)
        def _(level):
            number = level.astype(jnp.float32)
            mix = (mixing[0, level], mixing[1, level])
            for t in range(count):
                rows = slice(8 * t, 8 * t + 8)
                centre, easts, wests, norths, souths = [], [], [], [], []
                for f in range(4):
                    c = source[f, level, rows, :]
                    z = pltpu.roll(link[f, rows, :], width - 3 - 8 * (levels - 1) + 8 * level, 1)
                    centre.append(c)
                    easts.append(pltpu.roll(jnp.where(lane == 0, z, c), width - 1, 1))
                    wests.append(pltpu.roll(jnp.where(lane == width - 1, z, c), 1, 1))
                    if t < tiles - 1:
                        norths.append(flat[f, pl.ds(level * deep + 8 * t + 1, 8), :])
                    else:
                        wrapped = pltpu.roll(source[f, level, 0:8, :], 7, 0)
                        norths.append(jnp.where(row == 7, wrapped, pltpu.roll(c, 7, 0)))
                    if t > 0:
                        souths.append(flat[f, pl.ds(level * deep + 8 * t - 1, 8), :])
                    else:
                        wrapped = pltpu.roll(source[f, level, deep - 8 : deep, :], 1, 0)
                        souths.append(jnp.where(row == 0, wrapped, pltpu.roll(c, 1, 0)))
                factor = [table[m, rows, :] for m in range(6)]
                new = update(centre, easts, wests, norths, souths, factor, number, mix)
                for f in range(4):
                    store(f, level, t, new[f])
            if after is not None:
                after(level)

    def side_step(source, target):
        mix = (mixing[0, levels], mixing[1, levels])
        number = (levels - 1 - group).astype(jnp.float32)
        @pl.loop(0, tiles)
        def _(t):
            rows = pl.ds(pl.multiple_of(8 * t, 8), 8)
            prior = pl.ds(pl.multiple_of(lax.rem(t + tiles - 1, tiles) * 8, 8), 8)
            following = pl.ds(pl.multiple_of(lax.rem(t + 1, tiles) * 8, 8), 8)
            for side in range(2):
                centre = [source[side, f, rows, :] for f in range(4)]
                easts = [pltpu.roll(c, width - 1, 1) for c in centre]
                wests = [pltpu.roll(c, 1, 1) for c in centre]
                norths = [
                    jnp.where(
                        row == 7,
                        pltpu.roll(source[side, f, following, :], 7, 0),
                        pltpu.roll(centre[f], 7, 0),
                    )
                    for f in range(4)
                ]
                souths = [
                    jnp.where(
                        row == 0,
                        pltpu.roll(source[side, f, prior, :], 1, 0),
                        pltpu.roll(centre[f], 1, 0),
                    )
                    for f in range(4)
                ]
                factor = [side_metric[side, m, rows, :] for m in range(6)]
                new = update(centre, easts, wests, norths, souths, factor, number, mix)
                for f in range(4):
                    target[side, f, rows, :] = new[f]

    def join(source):
        @pl.loop(0, tiles)
        def _(t):
            rows = pl.ds(pl.multiple_of(t * 8, 8), 8)
            for f in range(4):
                link[f, rows, :] = jnp.where(within == 2, source[0, f, rows, :], source[1, f, rows, :])

    def into(buffer):
        def store(f, level, t, value):
            buffer[f, level, 8 * t : 8 * t + 8, :] = value
        return store

    def final(f, level, t, value):
        result[f, level, 8 * t : 8 * t + 8, :] = value

    join(sides)
    main_step(state, into(second), tiles)
    side_step(sides, sides_second)
    join(sides_second)
    main_step(second, into(third), tiles)
    side_step(sides_second, sides_third)
    join(sides_third)

    def leave(level):
        for f in range(4):
            pltpu.make_async_copy(result.at[f, level], outs[f].at[level], store_sem.at[f]).start()

    main_step(third, final, tiles - 1, leave)
    for f in range(4):
        pltpu.make_async_copy(result.at[f], outs[f], store_sem.at[f]).wait()


def on_device(
    potential_heat_state,
    saltiness_anomaly,
    first_current_component,
    second_current_component,
    bathymetry_layer_total,
    westeast_cell_extent,
    southnorth_cell_extent,
    planetary_vorticity,
    scalar_mixing_factor,
    momentum_mixing_factor,
):
    fields = (potential_heat_state, saltiness_anomaly, first_current_component, second_current_component)
    metrics = (bathymetry_layer_total, westeast_cell_extent, southnorth_cell_extent, planetary_vorticity)
    levels, height, width = potential_heat_state.shape
    f32 = jnp.float32
    message = 4 * RIM * levels + 16
    deep = height + 8
    flat = (levels * height, width)
    vmem = pl.BlockSpec(memory_space=pltpu.VMEM)
    anywhere = pl.BlockSpec(memory_space=pltpu.HBM)
    laid = pl.pallas_call(
        exchange,
        out_shape=(
            pltpu.VMEM((4, levels, deep, width), f32),
            pltpu.VMEM((6, deep, width), f32),
            pltpu.VMEM((2, 4, deep, width), f32),
            pltpu.VMEM((2, 6, deep, width), f32),
            pltpu.VMEM((2, levels + 1, 8, width), f32),
        ),
        in_specs=[anywhere] * 10,
        out_specs=[vmem] * 5,
        scratch_shapes=[
            pltpu.SMEM((levels,), f32),
            pltpu.SMEM((levels,), f32),
            pltpu.VMEM((4,) + flat, f32),
            pltpu.VMEM((3, height, width), f32),
            pltpu.VMEM((height, width), jnp.int32),
            pltpu.VMEM((4, deep, width), f32),
            pltpu.VMEM((message, width), f32),
            pltpu.VMEM((message, width), f32),
            pltpu.VMEM((2, 5, deep, width), f32),
            pltpu.VMEM((32, width), f32),
            pltpu.VMEM((32, width), f32),
            pltpu.VMEM((message, width), f32),
            pltpu.VMEM((message, width), f32),
            pltpu.VMEM((5, height, width), f32),
            pltpu.VMEM((2, 2, height, width), f32),
            pltpu.VMEM((2, 2, height, width), f32),
            pltpu.VMEM((32, width), f32),
            pltpu.VMEM((32, width), f32),
            pltpu.SemaphoreType.DMA((8,)),
            pltpu.SemaphoreType.DMA((8,)),
            pltpu.SemaphoreType.DMA((10,)),
        ],
        compiler_params=pltpu.CompilerParams(
            collective_id=0, has_side_effects=True, vmem_limit_bytes=int(60.6 * 2**20)
        ),
        name="exchange",
    )(*[x.reshape(flat) for x in fields], *metrics, scalar_mixing_factor, momentum_mixing_factor)
    news = pl.pallas_call(
        substeps,
        out_shape=(jax.ShapeDtypeStruct((levels, height, width), f32),) * 4,
        in_specs=[vmem] * 5,
        out_specs=[anywhere] * 4,
        scratch_shapes=[
            pltpu.VMEM((4, levels, deep, width), f32),
            pltpu.VMEM((4, levels, deep, width), f32),
            pltpu.VMEM((4, levels, height, width), f32),
            pltpu.VMEM((2, 4, deep, width), f32),
            pltpu.VMEM((2, 4, deep, width), f32),
            pltpu.VMEM((4, deep, width), f32),
            pltpu.SemaphoreType.DMA((4,)),
        ],
        compiler_params=pltpu.CompilerParams(vmem_limit_bytes=32 * 2**20),
        name="substeps",
    )(*laid)
    return tuple(news)


def solution(mesh):
    state, plane = P(None, "lat", "lon"), P("lat", "lon")
    return jax.shard_map(
        on_device,
        mesh=mesh,
        in_specs=(state,) * 4 + (plane,) * 4 + (P(), P()),
        out_specs=(state,) * 4,
        check_vma=False,
    )
```

```python
import functools

import jax
import jax.numpy as jnp
from jax import lax
from jax.experimental import pallas as pl
from jax.experimental.pallas import tpu as pltpu
from jax.sharding import PartitionSpec as P

STEPS = 3
RIM = 3
time_step = 0.2

MESH = pl.DeviceIdType.MESH


def lanes(shape):
    return lax.broadcasted_iota(jnp.int32, shape, len(shape) - 1)


def factors(bath, we, sn, vo):
    a, b = 1.0 / we, 1.0 / sn
    return (
        bath, time_step * a * a, time_step * b * b,
        0.5 * time_step * a, 0.5 * time_step * b, time_step * vo,
    )


def exchange(
    x0, x1, x2, x3, bathy, wide, high, vort, tracer_mix, momentum_mix,
    state, table, sides, side_metric, mixing,
    factor_t, factor_m, field, whole, bath, metric,
    rows_n, rows_s, strips, strip_n, strip_s,
    out_n, out_s, packed, to_side, from_side, edge_n, edge_s,
    send_sem, recv_sem, load_sem,
):
    levels, width = state.shape[1], state.shape[3]
    height = wide.shape[0]
    deep = height + 8
    lat, lon = lax.axis_index("lat"), lax.axis_index("lon")
    lats, lons = lax.axis_size("lat"), lax.axis_size("lon")
    last, bottom = lat == lats - 1, lat == 0
    east = (lat, lax.rem(lon + 1, lons))
    west = (lat, lax.rem(lon + lons - 1, lons))
    north = (
        jnp.where(last, lat, lat + 1),
        jnp.where(last, lons - 1 - lon, lon),
    )
    south = (lat - 1, lon)

    loads = [
        pltpu.make_async_copy(x, field.at[f], load_sem.at[f]) for f, x in enumerate((x0, x1, x2, x3))
    ]
    loads.append(pltpu.make_async_copy(bathy, bath, load_sem.at[4]))
    loads += [
        pltpu.make_async_copy(x, whole.at[m], load_sem.at[5 + m]) for m, x in enumerate((wide, high, vort))
    ]
    loads += [
        pltpu.make_async_copy(tracer_mix, factor_t, load_sem.at[8]),
        pltpu.make_async_copy(momentum_mix, factor_m, load_sem.at[9]),
    ]
    for load in loads:
        load.start()

    barrier = pltpu.get_barrier_semaphore()
    for peer in (east, west, north):
        pl.semaphore_signal(barrier, inc=1, device_id=peer, device_id_type=MESH)

    @pl.when(lat > 0)
    def _():
        pl.semaphore_signal(barrier, inc=1, device_id=south, device_id_type=MESH)

    lane = lanes((8, width))
    row = lax.broadcasted_iota(jnp.int32, (8, width), 0)
    group = lane // 8
    within = lane - group * 8

    def pack(pair, tile):
        start = pl.multiple_of(tile * 8, 8)
        rows = pl.ds(start, 8)
        cols = []
        for f in (2 * pair, 2 * pair + 1):
            acc = pltpu.roll(field[f, rows, :], 8 * (levels - 1) + RIM, 1)
            for level in range(1, levels):
                spot = levels - 1 - level
                at = pl.ds(pl.multiple_of(start + level * height, 8), 8)
                acc = jnp.where(group == spot, pltpu.roll(field[f, at, :], 8 * spot + RIM, 1), acc)
            packed[f, rows, :] = acc
            cols.append(acc)
        if pair == 0:
            acc = jnp.zeros((8, width), jnp.float32)
            raw = (bath[rows, :].astype(jnp.float32), whole[0, rows, :], whole[1, rows, :], whole[2, rows, :])
            for m in range(4):
                metric[m, rows, :] = raw[m]
                acc = jnp.where(group == m, pltpu.roll(raw[m], 8 * m + RIM, 1), acc)
            packed[4, rows, :] = acc
            extra_w = pltpu.roll(acc, 3, 1)
            extra_e = jnp.where(within == 3, extra_w, pltpu.roll(acc, 6, 1))
        else:
            extra_e = extra_w = pltpu.roll(packed[4, rows, :], 1, 1)
        one, two = cols
        to_side[0, pair, rows, :] = jnp.where(
            within < 3, one, jnp.where((within == 3) | (within == 7), extra_e, pltpu.roll(two, 4, 1))
        )
        to_side[1, pair, rows, :] = jnp.where(
            within < 3, pltpu.roll(two, width - 3, 1), jnp.where(within < 6, one, extra_w)
        )

    for at in (0, 1, 4, 5, 6, 7):
        loads[at].wait()

    @pl.loop(0, height // 8)
    def _(tile):
        pack(0, tile)

    @pl.when(lat > 0)
    def _():
        pl.semaphore_wait(barrier, 4)

    @pl.when(lat == 0)
    def _():
        pl.semaphore_wait(barrier, 3)

    def remote(src, dst, which, arrive, peer):
        return pltpu.make_async_remote_copy(
            src_ref=src, dst_ref=dst, send_sem=send_sem.at[which], recv_sem=recv_sem.at[arrive],
            device_id=peer, device_id_type=MESH,
        )

    across = []
    for pair in range(2):
        across.append(remote(to_side.at[0, pair], from_side.at[0, pair], 6 * pair, 6 * pair, east))
        across.append(remote(to_side.at[1, pair], from_side.at[1, pair], 6 * pair + 1, 6 * pair + 1, west))
    across[0].start()
    across[1].start()
    for at in (2, 3, 8, 9):
        loads[at].wait()

    @pl.loop(0, height // 8)
    def _(tile):
        pack(1, tile)

    across[2].start()
    across[3].start()

    def column(f, r, half):
        return field[f, pl.ds(r + half * 8 * height, 8, stride=height), :]

    for f in range(4):
        for r in range(RIM):
            at = (f * RIM + r) * levels
            for half in range(levels // 8):
                rows = slice(at + 8 * half, at + 8 * half + 8)
                out_s[rows, :] = column(f, r, half)
                out_n[rows, :] = column(f, height - RIM + r, half)
    base = 4 * RIM * levels
    out_s[base : base + 16, :] = jnp.zeros((16, width), jnp.float32)
    out_n[base : base + 16, :] = jnp.zeros((16, width), jnp.float32)
    for m in range(4):
        out_s[base + m * RIM : base + (m + 1) * RIM, :] = metric[m, 0:RIM, :]
        out_n[base + m * RIM : base + (m + 1) * RIM, :] = metric[m, height - RIM : height, :]

    def rows_out(to_n, to_s, recv_n, recv_s, first):
        up = remote(to_n, recv_s, first, first, north)
        fold = remote(to_n, recv_n, first, first + 1, north)
        down = remote(to_s, recv_n, first + 1, first + 1, south)

        @pl.when(last)
        def _():
            fold.start()

        @pl.when(lat < lats - 1)
        def _():
            up.start()

        @pl.when(lat > 0)
        def _():
            down.start()

        return up, down

    def rows_in(up, down):
        down.wait_recv()

        @pl.when(lat > 0)
        def _():
            up.wait_recv()

    def rows_sent(up, down):
        up.wait_send()

        @pl.when(lat > 0)
        def _():
            down.wait_send()

    @pl.when(lat == 0)
    def _():
        rows_s[...] = jnp.zeros(rows_s.shape, jnp.float32)
        strip_s[...] = jnp.zeros(strip_s.shape, jnp.float32)

    main = rows_out(out_n, out_s, rows_n, rows_s, 2)

    @pl.loop(0, height // 8)
    def _(tile):
        rows = pl.ds(pl.multiple_of(tile * 8, 8), 8)
        made = factors(*[metric[m, rows, :] for m in range(4)])
        for m in range(6):
            table[m, rows, :] = made[m]

    for copy in across:
        copy.wait_recv()

    @pl.loop(0, height // 8)
    def _(tile):
        rows = pl.ds(pl.multiple_of(tile * 8, 8), 8)
        for f in range(4):
            own = packed[f, rows, :]
            got_w = from_side[0, f // 2, rows, :]
            got_e = from_side[1, f // 2, rows, :]
            if f % 2 == 1:
                got_w = pltpu.roll(got_w, width - 4, 1)
                got_e = pltpu.roll(got_e, 3, 1)
            strips[0, f, rows, :] = jnp.where(within < RIM, got_w, own)
            strips[1, f, rows, :] = jnp.where(within < RIM, own, got_e)
        own = packed[4, rows, :]
        first, second = from_side[0, 0, rows, :], from_side[0, 1, rows, :]
        got_w = jnp.where(
            within == 0,
            pltpu.roll(first, width - 3, 1),
            jnp.where(within == 1, pltpu.roll(first, width - 6, 1), pltpu.roll(second, width - 1, 1)),
        )
        first, second = from_side[1, 0, rows, :], from_side[1, 1, rows, :]
        got_e = jnp.where(within < 5, pltpu.roll(first, width - 3, 1), pltpu.roll(second, width - 1, 1))
        strips[0, 4, rows, :] = jnp.where(within < RIM, got_w, own)
        strips[1, 4, rows, :] = jnp.where((within < RIM) | (within > 5), own, got_e)

    edge_n[30:32, :] = jnp.zeros((2, width), jnp.float32)
    edge_s[30:32, :] = jnp.zeros((2, width), jnp.float32)
    for side in range(2):
        for f in range(5):
            at = (side * 5 + f) * RIM
            edge_s[at : at + RIM, :] = strips[side, f, 0:RIM, :]
            edge_n[at : at + RIM, :] = strips[side, f, height - RIM : height, :]
    ends = rows_out(edge_n, edge_s, strip_n, strip_s, 4)

    @pl.loop(0, levels)
    def _(level):
        number = level.astype(jnp.float32)
        for t in range(height // 8):
            wet = table[0, 8 * t : 8 * t + 8, :] > number
            at = pl.ds(pl.multiple_of(level * height + 8 * t, 8), 8)
            for f in range(4):
                state[f, level, 8 * t : 8 * t + 8, :] = jnp.where(wet, field[f, at, :], 0.0)

    for k, mix in enumerate((factor_t, factor_m)):
        spread = jnp.zeros((8, width), jnp.float32)
        for level in range(levels):
            spread = jnp.where(group == levels - 1 - level, mix[level], spread)
            mixing[k, level] = jnp.full((8, width), mix[level], jnp.float32)
        mixing[k, levels] = spread

    def side_tables(rows):
        for side in range(2):
            mixed = strips[side, 4, rows, :]
            spread = []
            for m in range(4):
                value = jnp.where(group == m, mixed, 0.0)
                for hop in (8, 16, 32, 64):
                    value = value + pltpu.roll(value, hop, 1)
                spread.append(value)
            made = factors(*spread)
            for m in range(6):
                side_metric[side, m, rows, :] = made[m]
            wet = made[0] > (levels - 1 - group).astype(jnp.float32)
            for f in range(4):
                sides[side, f, rows, :] = jnp.where(wet, strips[side, f, rows, :], 0.0)

    @pl.loop(0, height // 8)
    def _(tile):
        side_tables(pl.ds(pl.multiple_of(tile * 8, 8), 8))

    for copy in across:
        copy.wait_send()
    rows_in(*main)

    def mirrored(value, index):
        pieces = [
            jnp.take_along_axis(value[i : i + 8, :], index, axis=1)
            for i in range(0, value.shape[0], 8)
        ]
        return jnp.concatenate(pieces, axis=0)

    signs = (1.0, 1.0, -1.0, -1.0)
    safe = (0.0, 1.0, 1.0, 0.0)
    turn = width - 1 - lane
    far, near = rows_n[base : base + 16, :], rows_s[base : base + 16, :]
    flipped = mirrored(far, turn)
    for m in range(4):
        metric[m, height:deep, :] = jnp.full((8, width), safe[m], jnp.float32)
        for k in range(RIM):
            at, fold = m * RIM + k, m * RIM + RIM - 1 - k
            metric[m, height + k : height + k + 1, :] = jnp.where(
                last, flipped[fold : fold + 1, :], far[at : at + 1, :]
            )
            metric[m, deep - RIM + k : deep - RIM + k + 1, :] = jnp.where(
                bottom, safe[m], near[at : at + 1, :]
            )
    made = factors(*[metric[m, height:deep, :] for m in range(4)])
    for m in range(6):
        table[m, height:deep, :] = made[m]
    for f in range(4):
        for k in range(RIM):
            at = (f * RIM + k) * levels
            fold = (f * RIM + RIM - 1 - k) * levels
            turned = signs[f] * mirrored(rows_n[fold : fold + levels, :], turn)
            state[f, :, height + k, :] = jnp.where(last, turned, rows_n[at : at + levels, :])
            state[f, :, deep - RIM + k, :] = rows_s[at : at + levels, :]
    rim = (row < RIM) | (row >= 8 - RIM)

    @pl.loop(0, levels)
    def _(level):
        wet = rim & (table[0, height:deep, :] > level.astype(jnp.float32))
        for f in range(4):
            state[f, level, height:deep, :] = jnp.where(wet, state[f, level, height:deep, :], 0.0)

    rows_in(*ends)
    side_far = strip_n[...]
    side_flipped = mirrored(side_far, group * 8 + jnp.where(within < 6, 5 - within, within))
    side_near = strip_s[...]
    for side in range(2):
        for f in range(5):
            if f == 4:
                fill = jnp.where((group == 1) | (group == 2), 1.0, 0.0)
            else:
                fill = jnp.zeros((8, width), jnp.float32)
            strips[side, f, height:deep, :] = fill
            for r in range(RIM):
                at = (side * 5 + f) * RIM + r
                fold = ((1 - side) * 5 + f) * RIM + RIM - 1 - r
                sign = 1.0 if f == 4 else signs[f]
                strips[side, f, height + r : height + r + 1, :] = jnp.where(
                    last, sign * side_flipped[fold : fold + 1, :], side_far[at : at + 1, :]
                )
                got = side_near[at : at + 1, :]
                if f == 4:
                    got = jnp.where(bottom, fill[0:1, :], got)
                strips[side, f, deep - RIM + r : deep - RIM + r + 1, :] = got
    side_tables(slice(height, deep))
    rows_sent(*main)
    rows_sent(*ends)


def substeps(
    state, table, sides, side_metric, mixing,
    y0, y1, y2, y3,
    second, third, result, sides_second, sides_third, link, store_sem,
):
    outs = (y0, y1, y2, y3)
    levels, deep, width = state.shape[1:]
    tiles = deep // 8
    lane = lanes((8, width))
    row = lax.broadcasted_iota(jnp.int32, (8, width), 0)
    group = lane // 8
    within = lane - group * 8

    def update(centre, easts, wests, norths, souths, factor, number, mix):
        bath, a2, b2, ah, bh, vo = factor
        wet = bath > number
        a2 = jnp.where(wet, a2, 0.0)
        b2 = jnp.where(wet, b2, 0.0)
        u, v = centre[2], centre[3]
        du, dv = u * ah, v * bh
        results = []
        for f in range(4):
            if f % 2 == 0:
                da, db = mix[f // 2] * a2, mix[f // 2] * b2
                ce, cw, cn, cs = da - du, da + du, db - dv, db + dv
                cc = 1.0 - 2.0 * (da + db)
            new = cc * centre[f] + (ce * easts[f] + cw * wests[f])
            new = new + (cn * norths[f] + cs * souths[f])
            if f == 2:
                new = new + vo * v
            if f == 3:
                new = new - vo * u
            results.append(new)
        return results

    def main_step(source, store, count, after=None):
        @pl.loop(0, levels)
        def _(level):
            number = level.astype(jnp.float32)
            mix = (mixing[0, level], mixing[1, level])
            for t in range(count):
                rows = slice(8 * t, 8 * t + 8)
                centre, easts, wests, norths, souths = [], [], [], [], []
                for f in range(4):
                    c = source[f, level, rows, :]
                    z = pltpu.roll(link[f, rows, :], width - 2 - 8 * (levels - 1) + 8 * level, 1)
                    centre.append(c)
                    easts.append(jnp.where(lane == width - 1, z, pltpu.roll(c, width - 1, 1)))
                    wests.append(jnp.where(lane == 0, z, pltpu.roll(c, 1, 1)))
                    if t < tiles - 1:
                        norths.append(source[f, level, 8 * t + 1 : 8 * t + 9, :])
                    else:
                        wrapped = pltpu.roll(source[f, level, 0:8, :], 7, 0)
                        norths.append(jnp.where(row == 7, wrapped, pltpu.roll(c, 7, 0)))
                    if t > 0:
                        souths.append(source[f, level, 8 * t - 1 : 8 * t + 7, :])
                    else:
                        wrapped = pltpu.roll(source[f, level, deep - 8 : deep, :], 1, 0)
                        souths.append(jnp.where(row == 0, wrapped, pltpu.roll(c, 1, 0)))
                factor = [table[m, rows, :] for m in range(6)]
                new = update(centre, easts, wests, norths, souths, factor, number, mix)
                for f in range(4):
                    store(f, level, t, new[f])
            if after is not None:
                after(level)

    def side_step(source, target):
        mix = (mixing[0, levels], mixing[1, levels])
        number = (levels - 1 - group).astype(jnp.float32)
        @pl.loop(0, tiles)
        def _(t):
            rows = pl.ds(pl.multiple_of(8 * t, 8), 8)
            prior = pl.ds(pl.multiple_of(lax.rem(t + tiles - 1, tiles) * 8, 8), 8)
            following = pl.ds(pl.multiple_of(lax.rem(t + 1, tiles) * 8, 8), 8)
            for side in range(2):
                centre = [source[side, f, rows, :] for f in range(4)]
                easts = [pltpu.roll(c, width - 1, 1) for c in centre]
                wests = [pltpu.roll(c, 1, 1) for c in centre]
                norths = [
                    jnp.where(
                        row == 7,
                        pltpu.roll(source[side, f, following, :], 7, 0),
                        pltpu.roll(centre[f], 7, 0),
                    )
                    for f in range(4)
                ]
                souths = [
                    jnp.where(
                        row == 0,
                        pltpu.roll(source[side, f, prior, :], 1, 0),
                        pltpu.roll(centre[f], 1, 0),
                    )
                    for f in range(4)
                ]
                factor = [side_metric[side, m, rows, :] for m in range(6)]
                new = update(centre, easts, wests, norths, souths, factor, number, mix)
                for f in range(4):
                    target[side, f, rows, :] = new[f]

    def join(source):
        @pl.loop(0, tiles)
        def _(t):
            rows = pl.ds(pl.multiple_of(t * 8, 8), 8)
            for f in range(4):
                beyond = pltpu.roll(source[1, f, rows, :], width - 2, 1)
                link[f, rows, :] = jnp.where(within == 2, source[0, f, rows, :], beyond)

    def into(buffer):
        def store(f, level, t, value):
            buffer[f, level, 8 * t : 8 * t + 8, :] = value
        return store

    def final(f, level, t, value):
        result[f, level, 8 * t : 8 * t + 8, :] = value

    join(sides)
    main_step(state, into(second), tiles)
    side_step(sides, sides_second)
    join(sides_second)
    main_step(second, into(third), tiles)
    side_step(sides_second, sides_third)
    join(sides_third)

    def leave(level):
        for f in range(4):
            pltpu.make_async_copy(result.at[f, level], outs[f].at[level], store_sem.at[f]).start()

    main_step(third, final, tiles - 1, leave)
    for f in range(4):
        pltpu.make_async_copy(result.at[f], outs[f], store_sem.at[f]).wait()


def on_device(
    potential_heat_state,
    saltiness_anomaly,
    first_current_component,
    second_current_component,
    bathymetry_layer_total,
    westeast_cell_extent,
    southnorth_cell_extent,
    planetary_vorticity,
    scalar_mixing_factor,
    momentum_mixing_factor,
):
    fields = (potential_heat_state, saltiness_anomaly, first_current_component, second_current_component)
    metrics = (bathymetry_layer_total, westeast_cell_extent, southnorth_cell_extent, planetary_vorticity)
    levels, height, width = potential_heat_state.shape
    f32 = jnp.float32
    message = 4 * RIM * levels + 16
    deep = height + 8
    flat = (levels * height, width)
    vmem = pl.BlockSpec(memory_space=pltpu.VMEM)
    anywhere = pl.BlockSpec(memory_space=pltpu.HBM)
    laid = pl.pallas_call(
        exchange,
        out_shape=(
            pltpu.VMEM((4, levels, deep, width), f32),
            pltpu.VMEM((6, deep, width), f32),
            pltpu.VMEM((2, 4, deep, width), f32),
            pltpu.VMEM((2, 6, deep, width), f32),
            pltpu.VMEM((2, levels + 1, 8, width), f32),
        ),
        in_specs=[anywhere] * 10,
        out_specs=[vmem] * 5,
        scratch_shapes=[
            pltpu.SMEM((levels,), f32),
            pltpu.SMEM((levels,), f32),
            pltpu.VMEM((4,) + flat, f32),
            pltpu.VMEM((3, height, width), f32),
            pltpu.VMEM((height, width), jnp.int32),
            pltpu.VMEM((4, deep, width), f32),
            pltpu.VMEM((message, width), f32),
            pltpu.VMEM((message, width), f32),
            pltpu.VMEM((2, 5, deep, width), f32),
            pltpu.VMEM((32, width), f32),
            pltpu.VMEM((32, width), f32),
            pltpu.VMEM((message, width), f32),
            pltpu.VMEM((message, width), f32),
            pltpu.VMEM((5, height, width), f32),
            pltpu.VMEM((2, 2, height, width), f32),
            pltpu.VMEM((2, 2, height, width), f32),
            pltpu.VMEM((32, width), f32),
            pltpu.VMEM((32, width), f32),
            pltpu.SemaphoreType.DMA((8,)),
            pltpu.SemaphoreType.DMA((8,)),
            pltpu.SemaphoreType.DMA((10,)),
        ],
        compiler_params=pltpu.CompilerParams(
            collective_id=0, has_side_effects=True, vmem_limit_bytes=int(60.6 * 2**20)
        ),
        name="exchange",
    )(*[x.reshape(flat) for x in fields], *metrics, scalar_mixing_factor, momentum_mixing_factor)
    news = pl.pallas_call(
        substeps,
        out_shape=(jax.ShapeDtypeStruct((levels, height, width), f32),) * 4,
        in_specs=[vmem] * 5,
        out_specs=[anywhere] * 4,
        scratch_shapes=[
            pltpu.VMEM((4, levels, deep, width), f32),
            pltpu.VMEM((4, levels, deep, width), f32),
            pltpu.VMEM((4, levels, height, width), f32),
            pltpu.VMEM((2, 4, deep, width), f32),
            pltpu.VMEM((2, 4, deep, width), f32),
            pltpu.VMEM((4, deep, width), f32),
            pltpu.SemaphoreType.DMA((4,)),
        ],
        compiler_params=pltpu.CompilerParams(vmem_limit_bytes=32 * 2**20),
        name="substeps",
    )(*laid)
    return tuple(news)


def solution(mesh):
    state, plane = P(None, "lat", "lon"), P("lat", "lon")
    return jax.shard_map(
        on_device,
        mesh=mesh,
        in_specs=(state,) * 4 + (plane,) * 4 + (P(), P()),
        out_specs=(state,) * 4,
        check_vma=False,
    )
```
